256 devices in a mesh: rows: 16 (over z, core), hid: 16 (over y, x).
Axes of the slice: x: 4, y: 4, z: 8, core: 2. Of those that a mesh axis runs over, the one named last changes fastest.
Arguments:
- q_latent: bfloat16 [512, 128, 512], P(('rows', 'hid')), may hold values from -450 to 450
- q_rope: bfloat16 [512, 64, 128], P(('rows', 'hid')), may hold values from -4 to 4
- latent_cache: bfloat16 [512, 3072, 512], P(('rows', 'hid')), may hold values from -8 to 8
- rope_cache: bfloat16 [512, 64, 3072], P(('rows', 'hid')), may hold values from -4 to 4
- indices: int32 [512, 2048], P(('rows', 'hid')), may hold values from 0 to 3071, as said below
- w_uv: bfloat16 [128, 512, 128], P('hid'), may hold values from -2 to 2
- w_out: bfloat16 [16384, 7168], P('hid', 'rows'), may hold values from -0.09375 to 0.09375
- residual: bfloat16 [512, 7168], P(None, 'rows'), may hold values from -64 to 64
- norm_gain: bfloat16 [7168], P('rows'), may hold values from 0.099609375 to 1.8984375
- w_gate: bfloat16 [7168, 18432], P('rows', 'hid'), may hold values from -0.0625 to 0.0625
- w_up: bfloat16 [7168, 18432], P('rows', 'hid'), may hold values from -0.0625 to 0.0625
- w_down: bfloat16 [18432, 7168], P('hid', 'rows'), may hold values from -0.046875 to 0.046875
Outputs:
- layer_out: bfloat16 [512, 7168], P('hid', 'rows')
The draws below stay inside these ranges and needn't reach their ends.
Inputs may be any that keep to these rules, and one draw needn't show every extreme that they name: Each query's 2048 indices are distinct rows of its own sequence's cache.
All inputs are finite; a program needn't handle non-finite values.
Results may differ from the reference program's by a relative error of at most 0.02.
Values may be sent and summed in bfloat16 or wider, within the bound.
No kernel may reach another device: no remote copies, remote signals or barrier semaphores. Data moves between devices by JAX's collectives and lax.ppermute only.
A program may use at most 64 MiB of HBM per device.

```python
import math
import jax
import jax.numpy as jnp
from jax import lax

D = 7168
FF = 18432
H = 128
LAT = 512
ROPE = 64
VDIM = 128
TOPK = 2048
CTX = 3072
BATCH = 512


def pick_rows(key):
    key = jax.random.fold_in(key, 11)
    row_keys = jax.random.split(key, BATCH)
    chosen = jax.vmap(lambda one_key: jax.random.permutation(one_key, CTX)[:TOPK])(row_keys)
    return chosen.astype(jnp.int32)


def draw_indices(key, part):
    return pick_rows(key)


def draw_latent_cache(key, part):
    key = jax.random.fold_in(key, 3)
    first_key = jax.random.fold_in(key, 0)
    base = jnp.clip(jax.random.normal(first_key, (BATCH, CTX, LAT), jnp.float32), -4.0, 4.0)
    return base.astype(jnp.bfloat16)


def draw_q_latent(key, part):
    key = jax.random.fold_in(key, 4)
    first_key = jax.random.fold_in(key, 0)
    base = jnp.clip(0.6 * jax.random.normal(first_key, (BATCH, H, LAT), jnp.float32), -4.0, 4.0)
    return base.astype(jnp.bfloat16)


def draw_residual(key, part):
    key = jax.random.fold_in(key, 5)
    first_key, second_key, third_key = jax.random.split(key, 3)
    base = jnp.clip(jax.random.normal(first_key, (BATCH, D), jnp.float32), -4.0, 4.0)
    row_scale = jnp.exp(jax.random.uniform(second_key, (BATCH, 1), jnp.float32, math.log(0.4), math.log(4.0)))
    col_scale = jnp.exp(jax.random.uniform(third_key, (1, D), jnp.float32, math.log(0.4), math.log(4.0)))
    return (base * row_scale * col_scale).astype(jnp.bfloat16)


def shard_levels(key, shape, cuts, smallest, top_value):
    level, own = 1.0, jax.random.fold_in(key, 6)
    for axis_at, parts in cuts:
        heights = jnp.exp(jax.random.uniform(jax.random.fold_in(own, axis_at), (parts,), jnp.float32, smallest / len(cuts), top_value / len(cuts)))
        level = level * jnp.repeat(heights, shape[axis_at] // parts).reshape([-1 if axis == axis_at else 1 for axis in range(len(shape))])
    return level


def bell_draw(key, shape, scale, most, cuts=(), kind=jnp.bfloat16):
    array = scale * jax.random.normal(key, shape, jnp.float32)
    if cuts:
        array = array * shard_levels(key, shape, cuts, -0.22, 0.18)
    return jnp.clip(array, -most, most).astype(kind)


def setup_inputs(seed: int = 0) -> dict:
    key_of = jax.random.split(jax.random.key(seed), 13)
    return {
        "q_latent": draw_q_latent(jax.random.fold_in(key_of[12], 71), 0),
        "q_rope": bell_draw(key_of[1], (BATCH, ROPE, H), 0.6, 4.0, ((0, 256),)),
        "latent_cache": draw_latent_cache(jax.random.fold_in(key_of[12], 71), 0),
        "rope_cache": bell_draw(key_of[3], (BATCH, ROPE, CTX), 1.0, 4.0, ((0, 256),)),
        "indices": draw_indices(jax.random.fold_in(key_of[12], 71), 0),
        "w_uv": bell_draw(key_of[5], (H, LAT, VDIM), (max(LAT // 64, 1)) ** -0.5, 2.0, ((0, 16),)),
        "w_out": bell_draw(key_of[6], (H * VDIM, D), (H * VDIM // 4) ** -0.5, 0.09375, ((0, 16), (1, 16))),
        "residual": draw_residual(jax.random.fold_in(key_of[12], 71), 0),
        "norm_gain": jnp.clip(1.0 + 0.18 * jax.random.normal(key_of[8], (D,), jnp.float32), 0.099609375, 1.8984375).astype(jnp.bfloat16),
        "w_gate": bell_draw(key_of[9], (D, FF), D ** -0.5, 0.0625, ((0, 16), (1, 16))),
        "w_up": bell_draw(key_of[10], (D, FF), D ** -0.5, 0.0625, ((0, 16), (1, 16))),
        "w_down": bell_draw(key_of[11], (FF, D), FF ** -0.5, 0.046875, ((0, 16), (1, 16))),
    }


def attend_row(query_lat, query_rope, lat_rows, rope_rows, chosen):
    picked = jnp.take(lat_rows, chosen, axis=0)
    picked_rope = jnp.take(rope_rows, chosen, axis=1)
    scores = jnp.dot(query_lat, picked.T, preferred_element_type=jnp.float32)
    scores = scores + jnp.dot(query_rope.T, picked_rope, preferred_element_type=jnp.float32)
    scores = scores * (1.0 / math.sqrt(VDIM + ROPE))
    weights = jax.nn.softmax(scores, axis=-1).astype(jnp.bfloat16)
    return jnp.dot(weights, picked, preferred_element_type=jnp.float32).astype(jnp.bfloat16)

def reference(q_latent, q_rope, latent_cache, rope_cache, indices, w_uv, w_out, residual, norm_gain, w_gate, w_up, w_down):
    context = lax.map(lambda item: attend_row(*item), (q_latent, q_rope, latent_cache, rope_cache, indices))
    heads_out = jnp.einsum('bhl,hlv->bhv', context.astype(jnp.float32), w_uv.astype(jnp.float32)).astype(jnp.bfloat16)
    flat_heads = heads_out.reshape(BATCH, H * VDIM)
    attn = jnp.dot(flat_heads, w_out, preferred_element_type=jnp.float32)
    mid = (residual.astype(jnp.float32) + attn).astype(jnp.bfloat16)
    mid_wide = mid.astype(jnp.float32)
    rstd = lax.rsqrt(lax.optimization_barrier(jnp.sum(mid_wide * mid_wide, axis=1)) / D + 1e-06)
    scaled = (mid_wide * norm_gain.astype(jnp.float32)).astype(jnp.bfloat16)
    gate = jnp.dot(scaled, w_gate, preferred_element_type=jnp.float32) * rstd[:, None]
    upper = jnp.dot(scaled, w_up, preferred_element_type=jnp.float32) * rstd[:, None]
    hidden = (jax.nn.silu(gate) * upper).astype(jnp.bfloat16)
    down = jnp.dot(hidden, w_down, preferred_element_type=jnp.float32)
    return (mid_wide + down).astype(jnp.bfloat16)
```

```python
import functools
import math

import jax
import jax.numpy as jnp
from jax import lax
from jax.experimental import pallas as pl
from jax.experimental.pallas import tpu as pltpu
from jax.sharding import Mesh
from jax.sharding import PartitionSpec as P

D = 7168
ROPE = 64
VDIM = 128
LAT = 512
HEADS = 128
CTX = 3072
F32 = jnp.float32
BF16 = jnp.bfloat16
HID = ("y", "x")
LAYER = ("core", "y", "x")
LANES = 128
EXP2_SCALE = math.log2(math.e) / math.sqrt(VDIM + ROPE)


def dot(a, b, dims=((1,), (0,))):
    return lax.dot_general(a, b, (dims, ((), ())), preferred_element_type=F32)


def iota(shape, dim):
    return lax.broadcasted_iota(jnp.int32, shape, dim)


def whole(n):
    return [pl.BlockSpec(memory_space=pltpu.VMEM)] * n


def smem():
    return pl.BlockSpec(memory_space=pltpu.SMEM)


def params(mib):
    return pltpu.CompilerParams(vmem_limit_bytes=mib * 2**20)


def cost(flops, nbytes):
    return pl.CostEstimate(flops=flops, bytes_accessed=nbytes, transcendentals=0)


def attend_kernel(idx_ref, ql_ref, qr_ref, lat_ref, rope_ref, out_ref, scores, both):
    seq = pl.program_id(0)
    idx = idx_ref[0]
    groups = CTX // LANES
    high = (iota((32, idx.shape[1]), 0) == lax.shift_right_logical(idx, 7)).astype(F32).astype(BF16)
    low = (iota((LANES, idx.shape[1]), 0) == (idx & 127)).astype(F32).astype(BF16)
    count = dot(high, low, ((1,), (1,)))
    bias = jnp.where(count > 0.5, 0.0, -1e30)

    q_lat = ql_ref[0]
    q_rope = qr_ref[0]
    step = 512
    top = jnp.full((HEADS, LANES), -3e38, F32)
    for at in range(0, CTX, step):
        part = dot(q_lat, lat_ref[0, at : at + step, :], ((1,), (1,)))
        part = part + dot(q_rope, rope_ref[0, :, at : at + step], ((0,), (0,)))
        for j in range(step // LANES):
            g = at // LANES + j
            piece = part[:, j * LANES : (j + 1) * LANES] + bias[g : g + 1, :]
            scores[:, g * LANES : (g + 1) * LANES] = piece
            top = jnp.maximum(top, piece)
    peak = jnp.max(top, axis=1, keepdims=True)
    total = jnp.zeros((HEADS, LANES), F32)
    acc = jnp.zeros((HEADS, LAT), F32)
    for at in range(0, CTX, step):
        e = jnp.exp2((scores[:, at : at + step] - peak) * EXP2_SCALE)
        for j in range(step // LANES):
            total = total + e[:, j * LANES : (j + 1) * LANES]
        acc = acc + dot(e.astype(BF16), lat_ref[0, at : at + step, :])
    norm = jnp.sum(total, axis=1, keepdims=True)
    both[pl.ds(pl.multiple_of(seq * HEADS, HEADS), HEADS), :] = (acc / norm).astype(BF16)

    @pl.when(seq == 1)
    def _():
        row = iota((256, 256), 0)
        col = iota((256, 256), 1)
        i, s, h, c = row & 3, (row >> 2) & 1, (row >> 3) & 15, row >> 7
        pick = (col == s * HEADS + h * 8 + c * 4 + i).astype(F32).astype(BF16)
        out_ref[...] = dot(pick, both[...]).astype(BF16)


def attend(idx, q_lat, q_rope, lat, rope):
    return pl.pallas_call(
        attend_kernel,
        grid=(2,),
        in_specs=[
            pl.BlockSpec((1, 1, idx.shape[2]), lambda s: (s, 0, 0)),
            pl.BlockSpec((1, HEADS, LAT), lambda s: (s, 0, 0)),
            pl.BlockSpec((1, ROPE, HEADS), lambda s: (s, 0, 0)),
            pl.BlockSpec((1, CTX, LAT), lambda s: (s, 0, 0)),
            pl.BlockSpec((1, ROPE, CTX), lambda s: (s, 0, 0)),
        ],
        out_specs=pl.BlockSpec((256, LAT), lambda s: (0, 0)),
        out_shape=jax.ShapeDtypeStruct((256, LAT), BF16),
        scratch_shapes=[pltpu.VMEM((HEADS, CTX), F32), pltpu.VMEM((256, LAT), BF16)],
        compiler_params=params(24),
        cost_estimate=cost(1_800_000_000, 8_000_000),
        name="attend",
    )(idx, q_lat, q_rope, lat, rope)


def heads_kernel(core_ref, x_ref, w_ref, out_ref):
    core = core_ref[0]
    row = iota((256, 256), 0)
    col = iota((256, 256), 1)
    pick = (col == (row & 63) * 4 + (row >> 6)).astype(F32).astype(BF16)
    sorted_rows = dot(pick, x_ref[...]).astype(BF16)
    for i in range(4):
        part = dot(sorted_rows[i * 64 : (i + 1) * 64], w_ref[core * 4 + i]).astype(BF16)
        for k in range(8):
            out_ref[k, :, i * VDIM : (i + 1) * VDIM] = part


def heads(core, x, w_uv):
    return pl.pallas_call(
        heads_kernel,
        in_specs=[smem()] + whole(2),
        out_specs=whole(1)[0],
        out_shape=jax.ShapeDtypeStruct((8, 64, 512), BF16),
        compiler_params=params(16),
        cost_estimate=cost(100_000_000, 2_000_000),
        name="heads",
    )(core, x, w_uv)


def project_kernel(core_ref, own_ref, other_ref, w_ref, out_ref):
    core = core_ref[0]
    mine = pl.ds(pl.multiple_of(core * 512, 512), 512)
    theirs = pl.ds(pl.multiple_of((1 - core) * 512, 512), 512)
    total = dot(own_ref[...], w_ref[mine, :]) + dot(other_ref[...], w_ref[theirs, :])
    out_ref[...] = total.astype(BF16)


def project(core, own, other, w_out):
    return pl.pallas_call(
        project_kernel,
        in_specs=[smem()] + whole(3),
        out_specs=whole(1)[0],
        out_shape=jax.ShapeDtypeStruct((512, w_out.shape[1]), BF16),
        compiler_params=params(16),
        cost_estimate=cost(470_000_000, 3_000_000),
        name="project",
    )(core, own, other, w_out)


def middle_kernel(place_ref, parts_ref, res_ref, gain_ref, mid_ref, out_ref):
    rows, cols = mid_ref.shape
    total = parts_ref[0].astype(F32)
    for k in range(1, parts_ref.shape[0]):
        total = total + parts_ref[k].astype(F32)
    res = res_ref[pl.ds(pl.multiple_of(place_ref[0] * rows, rows), rows), :]
    mid = (res.astype(F32) + total).astype(BF16)
    mid_ref[...] = mid
    wide = mid.astype(F32)
    squares = jnp.sum(wide * wide, axis=1, keepdims=True)
    upper = squares.astype(BF16).astype(F32)
    lane = iota((rows, 512 - cols), 1)
    extra = jnp.where(lane == 0, upper, jnp.where(lane == 1, squares - upper, 0.0)).astype(BF16)
    scaled = (wide * gain_ref[...].astype(F32)).astype(BF16)
    for k in range(out_ref.shape[0]):
        out_ref[k, :, :cols] = scaled
        out_ref[k, :, cols:] = extra


def middle(place, parts, residual, gain):
    rows, cols = parts.shape[1:]
    return pl.pallas_call(
        middle_kernel,
        in_specs=[smem()] + whole(3),
        out_specs=whole(2),
        out_shape=[
            jax.ShapeDtypeStruct((rows, cols), BF16),
            jax.ShapeDtypeStruct((16, rows, 512), BF16),
        ],
        compiler_params=params(16),
        cost_estimate=cost(1_000_000, 1_500_000),
        name="middle",
    )(place, parts, residual, gain)


def widen_kernel(core_ref, own_ref, other_ref, g_own, g_other, u_own, u_other, out_ref):
    core = core_ref[0]
    deep = g_own.shape[0]
    full = pl.ds(pl.multiple_of(core * 640, LANES), 512)
    own = own_ref[:, :deep]
    other = other_ref[:, :deep]
    chunk = out_ref.shape[1]

    def put(at, width, value):
        value = value.astype(BF16)
        for z in range(8):
            out_ref[z, :, at : at + width] = value[z * chunk : (z + 1) * chunk]

    put(0, 512, dot(own, g_own[:, full]) + dot(other, g_other[:, full]))
    put(512, 512, dot(own, u_own[:, full]) + dot(other, u_other[:, full]))
    gate = dot(own, g_own[:, 512:640]) + dot(other, g_other[:, 512:640])
    upper = dot(own, u_own[:, 512:640]) + dot(other, u_other[:, 512:640])
    first = core == 0
    straight = jnp.where(first, gate, upper)
    turned = pltpu.roll(jnp.where(first, upper, gate), 64, 1)
    lane = iota(gate.shape, 1)
    front = jnp.where(first, 64, 128)
    back = jnp.where(first, 0, 64)
    put(1024, LANES, jnp.where((lane >= back) & (lane < front), straight, turned))
    squares = jnp.sum(own_ref[:, deep:].astype(F32), axis=1, keepdims=True) + jnp.sum(
        other_ref[:, deep:].astype(F32), axis=1, keepdims=True
    )
    high = squares.astype(BF16).astype(F32)
    put(1152, LANES, jnp.where(lane == 0, high, jnp.where(lane == 1, squares - high, 0.0)))


def widen(core, own, other, *weights):
    return pl.pallas_call(
        widen_kernel,
        in_specs=[smem()] + whole(6),
        out_specs=whole(1)[0],
        out_shape=jax.ShapeDtypeStruct((8, 64, 1280), BF16),
        compiler_params=params(24),
        cost_estimate=cost(1_100_000_000, 6_000_000),
        name="widen",
    )(core, own, other, *weights)


def gated(gate, upper):
    return gate / (1.0 + jnp.exp(-gate)) * upper


def hidden_kernel(core_ref, parts_ref, out_ref):
    def total(at, width):
        value = parts_ref[0, :, at : at + width].astype(F32)
        for k in range(1, parts_ref.shape[0]):
            value = value + parts_ref[k, :, at : at + width].astype(F32)
        return value

    squares = jnp.sum(total(1152, LANES), axis=1, keepdims=True)
    rstd = lax.rsqrt(squares / D + 1e-06)
    full = gated(total(0, 512) * rstd, total(512, 512) * rstd).astype(BF16)
    mixed = total(1024, LANES) * rstd
    value = gated(mixed, pltpu.roll(mixed, 64, 1))
    first = core_ref[0] == 0
    lane = iota(value.shape, 1)
    begin = jnp.where(first, 0, 64)
    value = jnp.where(first, value, pltpu.roll(value, 64, 1))
    value = jnp.where((lane >= begin) & (lane < begin + 64), value, 0.0).astype(BF16)
    for k in range(out_ref.shape[0]):
        out_ref[k, :, :512] = full
        out_ref[k, :, 512:] = value


def make_hidden(core, parts):
    return pl.pallas_call(
        hidden_kernel,
        in_specs=[smem()] + whole(1),
        out_specs=whole(1)[0],
        out_shape=jax.ShapeDtypeStruct((8, 64, 640), BF16),
        compiler_params=params(16),
        cost_estimate=cost(5_000_000, 2_000_000),
        name="hidden",
    )(core, parts)


def down_kernel(core_ref, own_ref, other_ref, w_ref, out_ref):
    core = core_ref[0]
    mine = pl.ds(pl.multiple_of(core * 640, LANES), 512)
    theirs = pl.ds(pl.multiple_of((1 - core) * 640, LANES), 512)
    total = dot(own_ref[:, :512], w_ref[mine, :]) + dot(other_ref[:, :512], w_ref[theirs, :])
    total = total + dot(own_ref[:, 512:] + other_ref[:, 512:], w_ref[512:640, :])
    out_ref[...] = total.astype(BF16)


def down(core, own, other, w_down):
    return pl.pallas_call(
        down_kernel,
        in_specs=[smem()] + whole(3),
        out_specs=whole(1)[0],
        out_shape=jax.ShapeDtypeStruct((512, w_down.shape[1]), BF16),
        compiler_params=params(16),
        cost_estimate=cost(550_000_000, 3_500_000),
        name="down",
    )(core, own, other, w_down)


def last_kernel(parts_ref, mid_ref, out_ref):
    total = parts_ref[0].astype(F32)
    for k in range(1, parts_ref.shape[0]):
        total = total + parts_ref[k].astype(F32)
    out_ref[...] = (mid_ref[...].astype(F32) + total).astype(BF16)


def last(parts, mid):
    return pl.pallas_call(
        last_kernel,
        in_specs=whole(2),
        out_specs=whole(1)[0],
        out_shape=jax.ShapeDtypeStruct(mid.shape, BF16),
        compiler_params=params(16),
        cost_estimate=cost(1_000_000, 1_000_000),
        name="last",
    )(parts, mid)


def exchange(x, axes):
    return lax.all_to_all(x, axes, split_axis=0, concat_axis=0, tiled=True)


def swap(x):
    return lax.ppermute(x, "core", [(0, 1), (1, 0)])


def body(
    q_latent,
    q_rope,
    latent_cache,
    rope_cache,
    indices,
    w_uv,
    w_out,
    residual,
    norm_gain,
    w_gate,
    w_up,
    w_down,
):
    core = lax.axis_index("core").astype(jnp.int32).reshape(1)
    place = lax.axis_index(HID).astype(jnp.int32).reshape(1)
    gate_other = swap(w_gate)
    up_other = swap(w_up)

    context = attend(indices[:, None, :], q_latent, q_rope, latent_cache, rope_cache)
    moved = exchange(context.reshape(32, 8, LAT), LAYER).reshape(256, LAT)
    flat = exchange(heads(core, moved, w_uv), "z").reshape(512, 512)
    partial = project(core, flat, swap(flat), w_out)
    parts = exchange(partial.reshape(16, 32, -1), HID)
    mid, scaled = middle(place, parts, residual, norm_gain[None, :])
    scaled = exchange(scaled, HID).reshape(512, 512)
    wide = widen(core, scaled, swap(scaled), w_gate, gate_other, w_up, up_other)
    hidden = make_hidden(core, exchange(wide, "z"))
    hidden = exchange(hidden, "z").reshape(512, 640)
    outer = down(core, hidden, swap(hidden), w_down)
    return last(exchange(outer.reshape(16, 32, -1), HID), mid)


def solution(mesh):
    axes = Mesh(mesh.devices.reshape(8, 2, 4, 4), ("z", "core", "y", "x"))
    rows = ("z", "core")
    every = ("z", "core", "y", "x")
    placed = (
        P(every, None, None),
        P(every, None, None),
        P(every, None, None),
        P(every, None, None),
        P(every, None),
        P(HID, None, None),
        P(HID, rows),
        P(None, rows),
        P(rows),
        P(rows, HID),
        P(rows, HID),
        P(HID, rows),
    )
    return jax.shard_map(
        body, mesh=axes, in_specs=placed, out_specs=P(HID, rows), check_vma=False
    )
```

```python
import functools
import math

import jax
import jax.numpy as jnp
from jax import lax
from jax.experimental import pallas as pl
from jax.experimental.pallas import tpu as pltpu
from jax.sharding import Mesh
from jax.sharding import PartitionSpec as P

D = 7168
ROPE = 64
VDIM = 128
LAT = 512
HEADS = 128
CTX = 3072
F32 = jnp.float32
BF16 = jnp.bfloat16
HID = ("y", "x")
LAYER = ("core", "y", "x")
LANES = 128
EXP2_SCALE = math.log2(math.e) / math.sqrt(VDIM + ROPE)


def dot(a, b, dims=((1,), (0,))):
    return lax.dot_general(a, b, (dims, ((), ())), preferred_element_type=F32)


def iota(shape, dim):
    return lax.broadcasted_iota(jnp.int32, shape, dim)


def whole(n):
    return [pl.BlockSpec(memory_space=pltpu.VMEM)] * n


def smem():
    return pl.BlockSpec(memory_space=pltpu.SMEM)


def params(mib):
    return pltpu.CompilerParams(vmem_limit_bytes=mib * 2**20)


def cost(flops, nbytes):
    return pl.CostEstimate(flops=flops, bytes_accessed=nbytes, transcendentals=0)


def attend_kernel(idx_ref, ql_ref, qr_ref, lat_ref, rope_ref, out_ref, scores, both):
    seq = pl.program_id(0)
    idx = idx_ref[pl.ds(seq, 1), :]
    groups = CTX // LANES
    high = (iota((32, idx.shape[1]), 0) == lax.shift_right_logical(idx, 7)).astype(F32).astype(BF16)
    low = (iota((LANES, idx.shape[1]), 0) == (idx & 127)).astype(F32).astype(BF16)
    count = dot(high, low, ((1,), (1,)))
    bias = jnp.where(count > 0.5, 0.0, -1e30)

    q_lat = ql_ref[0]
    q_rope = qr_ref[0]
    step = 512
    top = jnp.full((HEADS, LANES), -3e38, F32)
    for at in range(0, CTX, step):
        part = dot(q_lat, lat_ref[0, at : at + step, :], ((1,), (1,)))
        part = part + dot(q_rope, rope_ref[0, :, at : at + step], ((0,), (0,)))
        for j in range(step // LANES):
            g = at // LANES + j
            piece = part[:, j * LANES : (j + 1) * LANES] + bias[g : g + 1, :]
            scores[:, g * LANES : (g + 1) * LANES] = piece
            top = jnp.maximum(top, piece)
    peak = jnp.max(top, axis=1, keepdims=True)
    total = jnp.zeros((HEADS, LANES), F32)
    acc = jnp.zeros((HEADS, LAT), F32)
    for at in range(0, CTX, step):
        e = jnp.exp2((scores[:, at : at + step] - peak) * EXP2_SCALE)
        for j in range(step // LANES):
            total = total + e[:, j * LANES : (j + 1) * LANES]
        acc = acc + dot(e.astype(BF16), lat_ref[0, at : at + step, :])
    norm = jnp.sum(total, axis=1, keepdims=True)
    both[pl.ds(pl.multiple_of(seq * HEADS, HEADS), HEADS), :] = (acc / norm).astype(BF16)

    @pl.when(seq == 1)
    def _():
        row = iota((256, 256), 0)
        col = iota((256, 256), 1)
        i, s, h, c = row & 3, (row >> 2) & 1, (row >> 3) & 15, row >> 7
        pick = (col == s * HEADS + h * 8 + c * 4 + i).astype(F32).astype(BF16)
        out_ref[...] = dot(pick, both[...]).astype(BF16)


def attend(idx, q_lat, q_rope, lat, rope):
    return pl.pallas_call(
        attend_kernel,
        grid=(2,),
        in_specs=[
            pl.BlockSpec(idx.shape, lambda s: (0, 0)),
            pl.BlockSpec((1, HEADS, LAT), lambda s: (s, 0, 0)),
            pl.BlockSpec((1, ROPE, HEADS), lambda s: (s, 0, 0)),
            pl.BlockSpec((1, CTX, LAT), lambda s: (s, 0, 0)),
            pl.BlockSpec((1, ROPE, CTX), lambda s: (s, 0, 0)),
        ],
        out_specs=pl.BlockSpec((256, LAT), lambda s: (0, 0)),
        out_shape=jax.ShapeDtypeStruct((256, LAT), BF16),
        scratch_shapes=[pltpu.VMEM((HEADS, CTX), F32), pltpu.VMEM((256, LAT), BF16)],
        compiler_params=params(58),
        cost_estimate=cost(1_800_000_000, 8_000_000),
        name="attend",
    )(idx, q_lat, q_rope, lat, rope)


def heads_kernel(core_ref, x_ref, w_ref, out_ref):
    core = core_ref[0]
    row = iota((256, 256), 0)
    col = iota((256, 256), 1)
    pick = (col == (row & 63) * 4 + (row >> 6)).astype(F32).astype(BF16)
    sorted_rows = dot(pick, x_ref[...]).astype(BF16)
    for i in range(4):
        part = dot(sorted_rows[i * 64 : (i + 1) * 64], w_ref[core * 4 + i]).astype(BF16)
        for k in range(8):
            out_ref[k, :, i * VDIM : (i + 1) * VDIM] = part


def heads(core, x, w_uv):
    return pl.pallas_call(
        heads_kernel,
        in_specs=[smem()] + whole(2),
        out_specs=whole(1)[0],
        out_shape=jax.ShapeDtypeStruct((8, 64, 512), BF16),
        compiler_params=params(16),
        cost_estimate=cost(100_000_000, 2_000_000),
        name="heads",
    )(core, x, w_uv)


def project_kernel(turn, core_ref, heads_ref, w_ref, *rest):
    half = core_ref[0] if turn == 0 else 1 - core_ref[0]
    rows = pl.ds(pl.multiple_of(half * 512, 512), 512)
    total = dot(heads_ref[...], w_ref[:, rows], ((1,), (1,)))
    if turn == 1:
        total = total + rest[0][...]
    rest[-1][...] = total.astype(rest[-1].dtype)


def project(core, own, w_out, before=None):
    turn = 0 if before is None else 1
    return pl.pallas_call(
        functools.partial(project_kernel, turn),
        in_specs=[smem()] + whole(2 + turn),
        out_specs=whole(1)[0],
        out_shape=jax.ShapeDtypeStruct((512, w_out.shape[0]), BF16 if turn else F32),
        compiler_params=params(16),
        cost_estimate=cost(240_000_000, 2_000_000),
        name="project" + "ab"[turn],
    )(core, own, w_out, *([before] if turn else []))


def middle_kernel(place_ref, parts_ref, res_ref, gain_ref, mid_ref, out_ref):
    rows, cols = mid_ref.shape
    total = parts_ref[0].astype(F32)
    for k in range(1, parts_ref.shape[0]):
        total = total + parts_ref[k].astype(F32)
    res = res_ref[pl.ds(pl.multiple_of(place_ref[0] * rows, rows), rows), :]
    mid = (res.astype(F32) + total).astype(BF16)
    mid_ref[...] = mid
    wide = mid.astype(F32)
    squares = jnp.sum(wide * wide, axis=1, keepdims=True)
    upper = squares.astype(BF16).astype(F32)
    lane = iota((rows, 512 - cols), 1)
    extra = jnp.where(lane == 0, upper, jnp.where(lane == 1, squares - upper, 0.0)).astype(BF16)
    scaled = (wide * gain_ref[...].astype(F32)).astype(BF16)
    for k in range(out_ref.shape[0]):
        out_ref[k, :, :cols] = scaled
        out_ref[k, :, cols:] = extra


def middle(place, parts, residual, gain):
    rows, cols = parts.shape[1:]
    return pl.pallas_call(
        middle_kernel,
        in_specs=[smem()] + whole(3),
        out_specs=whole(2),
        out_shape=[
            jax.ShapeDtypeStruct((rows, cols), BF16),
            jax.ShapeDtypeStruct((16, rows, 512), BF16),
        ],
        compiler_params=params(16),
        cost_estimate=cost(1_000_000, 1_500_000),
        name="middle",
    )(place, parts, residual, gain)


def first_kernel(core_ref, own_ref, g_ref, u_ref, out_ref):
    deep = g_ref.shape[0]
    full = pl.ds(pl.multiple_of(core_ref[0] * 640, LANES), 512)
    own = own_ref[:, :deep]
    out_ref[:, 0:512] = dot(own, g_ref[:, full])
    out_ref[:, 512:1024] = dot(own, u_ref[:, full])
    out_ref[:, 1024:1152] = dot(own, g_ref[:, 512:640])
    out_ref[:, 1152:1280] = dot(own, u_ref[:, 512:640])


def first(core, own, gate, upper):
    return pl.pallas_call(
        first_kernel,
        in_specs=[smem()] + whole(3),
        out_specs=whole(1)[0],
        out_shape=jax.ShapeDtypeStruct((512, 1280), F32),
        compiler_params=params(16),
        cost_estimate=cost(560_000_000, 5_000_000),
        name="first",
    )(core, own, gate, upper)


def widen_kernel(takes, core_ref, z_ref, part_ref, own_ref, other_ref, g_ref, u_ref, out_ref):
    deep = g_ref.shape[0]
    low = core_ref[0] == 0
    full = pl.ds(pl.multiple_of(core_ref[0] * 640, LANES), 512)
    wide = out_ref.dtype == F32

    def rows_of(ref, columns):
        pieces = []
        for far, begin, rows in takes:
            at = lax.rem(z_ref[0] + far, 8) * 64 + begin
            pieces.append(ref[pl.ds(pl.multiple_of(at, 32), rows), columns])
        return jnp.concatenate(pieces, axis=0)

    other = rows_of(other_ref, slice(0, deep))

    def put(block, value):
        value = value.astype(out_ref.dtype)
        at = source = 0
        for _, _, rows in takes:
            for j in range(value.shape[1] // LANES):
                begin = at + (block + j) * rows
                out_ref[begin : begin + rows] = value[
                    source : source + rows, j * LANES : (j + 1) * LANES
                ]
            at += 9 * rows + 16
            source += rows

    put(0, rows_of(part_ref, slice(0, 512)) + dot(other, g_ref[:, full]))
    put(4, rows_of(part_ref, slice(512, 1024)) + dot(other, u_ref[:, full]))
    gate = rows_of(part_ref, slice(1024, 1152)) + dot(other, g_ref[:, 512:640])
    upper = rows_of(part_ref, slice(1152, 1280)) + dot(other, u_ref[:, 512:640])
    straight = jnp.where(low, gate, upper)
    turned = pltpu.roll(jnp.where(low, upper, gate), 64, 1)
    lane = iota(gate.shape, 1)
    begin = jnp.where(low, 0, 64)
    put(8, jnp.where((lane >= begin) & (lane < begin + 64), straight, turned))
    extra = slice(deep, 512)
    squares = jnp.sum(rows_of(own_ref, extra).astype(F32), axis=1, keepdims=True)
    squares = squares + jnp.sum(rows_of(other_ref, extra).astype(F32), axis=1, keepdims=True)
    at = source = 0
    for _, first_row, rows in takes:
        same = iota((rows, LANES), 0) + first_row == iota((rows, LANES), 1)
        line = jnp.where(same, squares[source : source + rows], 0.0)
        line = jnp.sum(line, axis=0, keepdims=True)
        out_ref[at + 9 * rows : at + 9 * rows + 16] = tile_of(line, wide).astype(out_ref.dtype)
        at += 9 * rows + 16
        source += rows


def tile_of(line, wide):
    row = iota((16, LANES), 0)
    high = line if wide else line.astype(BF16).astype(F32)
    return jnp.where(row == 0, high, jnp.where(row == 1, line - high, 0.0))


def widen(takes, kind, core, z, part, own, other, gate, upper):
    rows = sum(9 * n + 16 for _, _, n in takes)
    return pl.pallas_call(
        functools.partial(widen_kernel, takes),
        in_specs=[smem(), smem()] + whole(5),
        out_specs=whole(1)[0],
        out_shape=jax.ShapeDtypeStruct((rows, LANES), kind),
        compiler_params=params(16),
        cost_estimate=cost(200_000_000, 6_000_000),
        name="widen",
    )(core, z, part, own, other, gate, upper)


BLOCK = 592
TO_LOWER = ((7, 0, 64), (2, 0, 64), (4, 0, 32))
TO_UPPER = ((1, 0, 64), (6, 0, 64), (4, 32, 32))
TO_KEEP = ((0, 0, 64), (5, 0, 64), (3, 0, 64))


def merge_kernel(keep_ref, above_ref, below_ref, stay_ref, down_ref, up_ref):
    def block(ref, k):
        return ref[k * BLOCK : (k + 1) * BLOCK].astype(F32)

    stay_ref[...] = block(keep_ref, 0) + block(above_ref, 0) + block(below_ref, 0)
    for out_ref, k, full_ref, half_ref, shift in (
        (down_ref, 1, below_ref, above_ref, 0),
        (up_ref, 2, above_ref, below_ref, 32),
    ):
        total = block(keep_ref, k) + block(full_ref, 1)
        half = half_ref[2 * BLOCK :].astype(F32)
        for j in range(9):
            at = j * 64
            out_ref[at + 32 - shift : at + 64 - shift] = total[
                at + 32 - shift : at + 64 - shift
            ].astype(BF16)
            value = total[at + shift : at + shift + 32] + half[j * 32 : (j + 1) * 32]
            out_ref[at + shift : at + shift + 32] = value.astype(BF16)
        line = jnp.sum(total[576:592] + half[288:304], axis=0, keepdims=True)
        out_ref[576:592] = tile_of(line, False).astype(BF16)


def merge(keep, above, below):
    shapes = [jax.ShapeDtypeStruct((BLOCK, LANES), kind) for kind in (F32, BF16, BF16)]
    return pl.pallas_call(
        merge_kernel,
        in_specs=whole(3),
        out_specs=whole(3),
        out_shape=shapes,
        compiler_params=params(16),
        cost_estimate=cost(5_000_000, 3_000_000),
        name="merge",
    )(keep, above, below)


def gated(gate, upper):
    return gate / (1.0 + jnp.exp(-gate)) * upper


def hidden_kernel(stay_ref, above_ref, below_ref, out_ref):
    chunk = 64

    def total(at, rows):
        value = above_ref[at : at + rows].astype(F32) + below_ref[at : at + rows].astype(F32)
        return stay_ref[at : at + rows] + value

    line = jnp.sum(total(576, 16), axis=0, keepdims=True)
    same = iota((chunk, LANES), 0) == iota((chunk, LANES), 1)
    squares = jnp.sum(jnp.where(same, line, 0.0), axis=1, keepdims=True)
    rstd = lax.rsqrt(squares / D + 1e-06)

    def put(at, value):
        value = value.astype(BF16)
        for k in range(out_ref.shape[0]):
            out_ref[k, at : at + value.shape[0]] = value

    for j in range(4):
        gate = total(j * chunk, chunk) * rstd
        put(j * chunk, gated(gate, total((4 + j) * chunk, chunk) * rstd))
    mixed = total(8 * chunk, chunk) * rstd
    value = gated(mixed, pltpu.roll(mixed, 64, 1))
    lane = iota((32, LANES), 1)
    put(256, jnp.where(lane < 64, value[:32], pltpu.roll(value[32:], 64, 1)))


def make_hidden(stay, above, below):
    return pl.pallas_call(
        hidden_kernel,
        in_specs=whole(3),
        out_specs=whole(1)[0],
        out_shape=jax.ShapeDtypeStruct((8, 288, LANES), BF16),
        compiler_params=params(16),
        cost_estimate=cost(5_000_000, 2_000_000),
        name="hidden",
    )(stay, above, below)


def down_kernel(turn, core_ref, units_ref, w_ref, *rest):
    core = core_ref[0] if turn == 0 else 1 - core_ref[0]
    low = core == 0
    rows = pl.ds(pl.multiple_of(core * 640, LANES), 512)
    blocks = [units_ref[:, j * 64 : (j + 1) * 64].reshape(512, LANES) for j in range(4)]
    total = dot(jnp.concatenate(blocks, axis=1), w_ref[:, rows], ((1,), (1,)))
    packed = units_ref[:, 256:288].astype(F32).reshape(256, LANES)
    turned = pltpu.roll(packed, 64, 1)
    lane = iota(packed.shape, 1)
    begin = jnp.where(low, 0, 64)
    here = (lane >= begin) & (lane < begin + 64)
    top = jnp.where(here, jnp.where(low, packed, turned), 0.0).reshape(8, 32, LANES)
    bottom = jnp.where(here, jnp.where(low, turned, packed), 0.0).reshape(8, 32, LANES)
    mixed = jnp.concatenate([top, bottom], axis=1).reshape(512, LANES).astype(BF16)
    total = total + dot(mixed, w_ref[:, 512:640], ((1,), (1,)))
    if turn == 1:
        total = total + rest[0][...]
    rest[-1][...] = total.astype(rest[-1].dtype)


def down(core, units, w_down, before=None):
    turn = 0 if before is None else 1
    return pl.pallas_call(
        functools.partial(down_kernel, turn),
        in_specs=[smem()] + whole(2 + turn),
        out_specs=whole(1)[0],
        out_shape=jax.ShapeDtypeStruct((512, w_down.shape[0]), BF16 if turn else F32),
        compiler_params=params(16),
        cost_estimate=cost(280_000_000, 2_000_000),
        name="down" + "ab"[turn],
    )(core, units, w_down, *([before] if turn else []))


def last_kernel(parts_ref, mid_ref, out_ref):
    total = parts_ref[0].astype(F32)
    for k in range(1, parts_ref.shape[0]):
        total = total + parts_ref[k].astype(F32)
    out_ref[...] = (mid_ref[...].astype(F32) + total).astype(BF16)


def last(parts, mid):
    return pl.pallas_call(
        last_kernel,
        in_specs=whole(2),
        out_specs=whole(1)[0],
        out_shape=jax.ShapeDtypeStruct(mid.shape, BF16),
        compiler_params=params(16),
        cost_estimate=cost(1_000_000, 1_000_000),
        name="last",
    )(parts, mid)


def exchange(x, axes):
    return lax.all_to_all(x, axes, split_axis=0, concat_axis=0, tiled=True)


def swap(x):
    return lax.ppermute(x, "core", [(0, 1), (1, 0)])


def shift(x, far):
    return lax.ppermute(x, "z", [(i, (i + far) % 8) for i in range(8)])


def body(
    q_latent,
    q_rope,
    latent_cache,
    rope_cache,
    indices,
    w_uv,
    w_out,
    residual,
    norm_gain,
    w_gate,
    w_up,
    w_down,
):
    core = lax.axis_index("core").astype(jnp.int32).reshape(1)
    place = lax.axis_index(HID).astype(jnp.int32).reshape(1)
    height = lax.axis_index("z").astype(jnp.int32).reshape(1)
    gate_other = swap(w_gate)
    up_other = swap(w_up)

    context = attend(indices, q_latent, q_rope, latent_cache, rope_cache)
    moved = exchange(context.reshape(32, 8, LAT), LAYER).reshape(256, LAT)
    flat = exchange(heads(core, moved, w_uv), "z").reshape(512, 512)
    other = swap(flat)
    partial = project(core, other, w_out.T, project(core, flat, w_out.T))
    parts = exchange(partial.reshape(16, 32, -1), HID)
    mid, scaled = middle(place, parts, residual, norm_gain[None, :])
    scaled = exchange(scaled, HID).reshape(512, 512)
    scaled_other = swap(scaled)
    part = first(core, scaled, w_gate, w_up)
    rest = (core, height, part, scaled, scaled_other, gate_other, up_other)
    from_above = shift(widen(TO_LOWER, BF16, *rest), 7)
    from_below = shift(widen(TO_UPPER, BF16, *rest), 1)
    stay, lower, upper = merge(widen(TO_KEEP, F32, *rest), from_above, from_below)
    hidden = exchange(make_hidden(stay, shift(lower, 5), shift(upper, 3)), "z")
    other = swap(hidden)
    outer = down(core, other, w_down.T, down(core, hidden, w_down.T))
    return last(exchange(outer.reshape(16, 32, -1), HID), mid)


def solution(mesh):
    axes = Mesh(mesh.devices.reshape(8, 2, 4, 4), ("z", "core", "y", "x"))
    rows = ("z", "core")
    every = ("z", "core", "y", "x")
    placed = (
        P(every, None, None),
        P(every, None, None),
        P(every, None, None),
        P(every, None, None),
        P(every, None),
        P(HID, None, None),
        P(HID, rows),
        P(None, rows),
        P(rows),
        P(rows, HID),
        P(rows, HID),
        P(HID, rows),
    )
    return jax.shard_map(
        body, mesh=axes, in_specs=placed, out_specs=P(HID, rows), check_vma=False
    )
```

```python
import functools
import math

import jax
import jax.numpy as jnp
from jax import lax
from jax.experimental import pallas as pl
from jax.experimental.pallas import tpu as pltpu
from jax.sharding import Mesh
from jax.sharding import PartitionSpec as P

D = 7168
ROPE = 64
VDIM = 128
LAT = 512
HEADS = 128
CTX = 3072
F32 = jnp.float32
BF16 = jnp.bfloat16
HID = ("y", "x")
LAYER = ("core", "y", "x")
LANES = 128
FAR = (0, 1, 7, 2, 6, 3, 5, 4)
EXP2_SCALE = math.log2(math.e) / math.sqrt(VDIM + ROPE)


def dot(a, b, dims=((1,), (0,))):
    return lax.dot_general(a, b, (dims, ((), ())), preferred_element_type=F32)


def iota(shape, dim):
    return lax.broadcasted_iota(jnp.int32, shape, dim)


def whole(n):
    return [pl.BlockSpec(memory_space=pltpu.VMEM)] * n


def smem():
    return pl.BlockSpec(memory_space=pltpu.SMEM)


def params(mib):
    return pltpu.CompilerParams(vmem_limit_bytes=mib * 2**20)


def cost(flops, nbytes):
    return pl.CostEstimate(flops=flops, bytes_accessed=nbytes, transcendentals=0)


def attend_kernel(idx_ref, ql_ref, qr_ref, lat_ref, rope_ref, out_ref, scores, both):
    seq = pl.program_id(0)
    idx = idx_ref[pl.ds(seq, 1), :]
    high = (iota((32, idx.shape[1]), 0) == lax.shift_right_logical(idx, 7)).astype(F32).astype(BF16)
    low = (iota((LANES, idx.shape[1]), 0) == (idx & 127)).astype(F32).astype(BF16)
    bias = jnp.where(dot(low, high, ((1,), (1,))) > 0.5, 0.0, -1e30)

    q_lat = ql_ref[0]
    q_rope = qr_ref[0]
    step = 1024
    top = jnp.full((8, HEADS), -3e38, F32)
    for at in range(0, CTX, step):
        part = dot(lat_ref[0, at : at + step, :], q_lat, ((1,), (1,)))
        part = part + dot(rope_ref[0, :, at : at + step], q_rope, ((0,), (0,)))
        for j in range(step // LANES):
            g = at // LANES + j
            piece = part[j * LANES : (j + 1) * LANES] + bias[:, g : g + 1]
            scores[g * LANES : (g + 1) * LANES, :] = piece
            top = jnp.maximum(top, jnp.max(piece.reshape(16, 8, HEADS), axis=0))
    peak = jnp.max(top, axis=0, keepdims=True)
    total = jnp.zeros((8, HEADS), F32)
    acc = jnp.zeros((HEADS, LAT), F32)
    for at in range(0, CTX, step):
        e = jnp.exp2((scores[at : at + step, :] - peak) * EXP2_SCALE)
        total = total + jnp.sum(e.reshape(step // 8, 8, HEADS), axis=0)
        acc = acc + dot(e.astype(BF16), lat_ref[0, at : at + step, :], ((0,), (0,)))
    norm = jnp.sum(total, axis=0, keepdims=True)
    same = iota((HEADS, HEADS), 0) == iota((HEADS, HEADS), 1)
    norm = jnp.sum(jnp.where(same, norm, 0.0), axis=1, keepdims=True)
    both[pl.ds(pl.multiple_of(seq * HEADS, HEADS), HEADS), :] = (acc / norm).astype(BF16)

    @pl.when(seq == 1)
    def _():
        row = iota((256, 256), 0)
        col = iota((256, 256), 1)
        i, s, h, c = row & 3, (row >> 2) & 1, (row >> 3) & 15, row >> 7
        pick = (col == s * HEADS + h * 8 + c * 4 + i).astype(F32).astype(BF16)
        out_ref[...] = dot(pick, both[...]).astype(BF16)


def attend(idx, q_lat, q_rope, lat, rope):
    return pl.pallas_call(
        attend_kernel,
        grid=(2,),
        in_specs=[
            pl.BlockSpec(idx.shape, lambda s: (0, 0)),
            pl.BlockSpec((1, HEADS, LAT), lambda s: (s, 0, 0)),
            pl.BlockSpec((1, ROPE, HEADS), lambda s: (s, 0, 0)),
            pl.BlockSpec((1, CTX, LAT), lambda s: (s, 0, 0)),
            pl.BlockSpec((1, ROPE, CTX), lambda s: (s, 0, 0)),
        ],
        out_specs=pl.BlockSpec((256, LAT), lambda s: (0, 0)),
        out_shape=jax.ShapeDtypeStruct((256, LAT), BF16),
        scratch_shapes=[pltpu.VMEM((CTX, HEADS), F32), pltpu.VMEM((256, LAT), BF16)],
        compiler_params=params(58),
        cost_estimate=cost(1_800_000_000, 8_000_000),
        name="attend",
    )(idx, q_lat, q_rope, lat, rope)


def heads_kernel(core_ref, x_ref, w_ref, out_ref):
    core = core_ref[0]
    row = iota((256, 256), 0)
    col = iota((256, 256), 1)
    pick = (col == (row & 63) * 4 + (row >> 6)).astype(F32).astype(BF16)
    sorted_rows = dot(pick, x_ref[...]).astype(BF16)
    for i in range(4):
        part = dot(sorted_rows[i * 64 : (i + 1) * 64], w_ref[core * 4 + i]).astype(BF16)
        out_ref[:, i * VDIM : (i + 1) * VDIM] = part


def heads(core, x, w_uv):
    return pl.pallas_call(
        heads_kernel,
        in_specs=[smem()] + whole(2),
        out_specs=whole(1)[0],
        out_shape=jax.ShapeDtypeStruct((64, 512), BF16),
        compiler_params=params(16),
        cost_estimate=cost(100_000_000, 2_000_000),
        name="heads",
    )(core, x, w_uv)


def pack_kernel(*refs):
    rows = refs[0].shape[0]
    for k, ref in enumerate(refs[:-1]):
        refs[-1][k * rows : (k + 1) * rows] = ref[...]


def pack(blocks):
    rows, columns = blocks[0].shape
    return pl.pallas_call(
        pack_kernel,
        in_specs=whole(8),
        out_specs=whole(1)[0],
        out_shape=jax.ShapeDtypeStruct((8 * rows, columns), BF16),
        compiler_params=params(16),
        cost_estimate=cost(0, 1_000_000),
        name="pack",
    )(*blocks)


def place_chunks(out_ref, z, value):
    for k, far in enumerate(FAR):
        at = pl.multiple_of(lax.rem(z + far, 8) * 64, 64)
        out_ref[pl.ds(at, 64), :] = value[k * 64 : (k + 1) * 64].astype(out_ref.dtype)


def project_kernel(turn, core_ref, z_ref, heads_ref, w_ref, *rest):
    half = core_ref[0] if turn == 0 else 1 - core_ref[0]
    rows = pl.ds(pl.multiple_of(half * 512, 512), 512)
    total = dot(heads_ref[...], w_ref[:, rows], ((1,), (1,)))
    if turn == 1:
        place_chunks(rest[1], z_ref[0], total + rest[0][...])
    else:
        rest[0][...] = total


def project(core, z, own, w_out, before=None):
    turn = 0 if before is None else 1
    return pl.pallas_call(
        functools.partial(project_kernel, turn),
        in_specs=[smem(), smem()] + whole(2 + turn),
        out_specs=whole(1)[0],
        out_shape=jax.ShapeDtypeStruct((512, w_out.shape[0]), BF16 if turn else F32),
        compiler_params=params(16),
        cost_estimate=cost(240_000_000, 2_000_000),
        name="project" + "ab"[turn],
    )(core, z, own, w_out, *([before] if turn else []))


def middle_kernel(place_ref, parts_ref, res_ref, gain_ref, mid_ref, out_ref):
    rows, cols = mid_ref.shape
    total = parts_ref[0].astype(F32)
    for k in range(1, parts_ref.shape[0]):
        total = total + parts_ref[k].astype(F32)
    res = res_ref[pl.ds(pl.multiple_of(place_ref[0] * rows, rows), rows), :]
    mid = (res.astype(F32) + total).astype(BF16)
    mid_ref[...] = mid
    wide = mid.astype(F32)
    squares = jnp.sum(wide * wide, axis=1, keepdims=True)
    upper = squares.astype(BF16).astype(F32)
    lane = iota((rows, 512 - cols), 1)
    extra = jnp.where(lane == 0, upper, jnp.where(lane == 1, squares - upper, 0.0)).astype(BF16)
    scaled = (wide * gain_ref[...].astype(F32)).astype(BF16)
    for k in range(out_ref.shape[0]):
        out_ref[k, :, :cols] = scaled
        out_ref[k, :, cols:] = extra


def middle(place, parts, residual, gain):
    rows, cols = parts.shape[1:]
    return pl.pallas_call(
        middle_kernel,
        in_specs=[smem()] + whole(3),
        out_specs=whole(2),
        out_shape=[
            jax.ShapeDtypeStruct((rows, cols), BF16),
            jax.ShapeDtypeStruct((16, rows, 512), BF16),
        ],
        compiler_params=params(16),
        cost_estimate=cost(1_000_000, 1_500_000),
        name="middle",
    )(place, parts, residual, gain)


def first_kernel(core_ref, own_ref, g_ref, u_ref, out_ref):
    deep = g_ref.shape[0]
    full = pl.ds(pl.multiple_of(core_ref[0] * 640, LANES), 512)
    own = own_ref[:, :deep]
    out_ref[:, 0:512] = dot(own, g_ref[:, full])
    out_ref[:, 512:1024] = dot(own, u_ref[:, full])
    out_ref[:, 1024:1152] = dot(own, g_ref[:, 512:640])
    out_ref[:, 1152:1280] = dot(own, u_ref[:, 512:640])


def first(core, own, gate, upper):
    return pl.pallas_call(
        first_kernel,
        in_specs=[smem()] + whole(3),
        out_specs=whole(1)[0],
        out_shape=jax.ShapeDtypeStruct((512, 1280), F32),
        compiler_params=params(16),
        cost_estimate=cost(560_000_000, 5_000_000),
        name="first",
    )(core, own, gate, upper)


def widen_kernel(takes, core_ref, z_ref, part_ref, own_ref, other_ref, g_ref, u_ref, out_ref):
    deep = g_ref.shape[0]
    low = core_ref[0] == 0
    full = pl.ds(pl.multiple_of(core_ref[0] * 640, LANES), 512)
    wide = out_ref.dtype == F32

    def rows_of(ref, columns):
        pieces = []
        for far, begin, rows in takes:
            at = lax.rem(z_ref[0] + far, 8) * 64 + begin
            pieces.append(ref[pl.ds(pl.multiple_of(at, 32), rows), columns])
        return jnp.concatenate(pieces, axis=0)

    other = rows_of(other_ref, slice(0, deep))

    def put(block, value):
        value = value.astype(out_ref.dtype)
        at = source = 0
        for _, _, rows in takes:
            for j in range(value.shape[1] // LANES):
                begin = at + (block + j) * rows
                out_ref[begin : begin + rows] = value[
                    source : source + rows, j * LANES : (j + 1) * LANES
                ]
            at += 9 * rows + 16
            source += rows

    put(0, rows_of(part_ref, slice(0, 512)) + dot(other, g_ref[:, full]))
    put(4, rows_of(part_ref, slice(512, 1024)) + dot(other, u_ref[:, full]))
    gate = rows_of(part_ref, slice(1024, 1152)) + dot(other, g_ref[:, 512:640])
    upper = rows_of(part_ref, slice(1152, 1280)) + dot(other, u_ref[:, 512:640])
    straight = jnp.where(low, gate, upper)
    turned = pltpu.roll(jnp.where(low, upper, gate), 64, 1)
    lane = iota(gate.shape, 1)
    begin = jnp.where(low, 0, 64)
    put(8, jnp.where((lane >= begin) & (lane < begin + 64), straight, turned))
    extra = slice(deep, 512)
    squares = jnp.sum(rows_of(own_ref, extra).astype(F32), axis=1, keepdims=True)
    squares = squares + jnp.sum(rows_of(other_ref, extra).astype(F32), axis=1, keepdims=True)
    at = source = 0
    for _, first_row, rows in takes:
        same = iota((rows, LANES), 0) + first_row == iota((rows, LANES), 1)
        line = jnp.where(same, squares[source : source + rows], 0.0)
        line = jnp.sum(line, axis=0, keepdims=True)
        out_ref[at + 9 * rows : at + 9 * rows + 16] = tile_of(line, wide).astype(out_ref.dtype)
        at += 9 * rows + 16
        source += rows


def tile_of(line, wide):
    row = iota((16, LANES), 0)
    high = line if wide else line.astype(BF16).astype(F32)
    return jnp.where(row == 0, high, jnp.where(row == 1, line - high, 0.0))


def widen(takes, kind, core, z, part, own, other, gate, upper):
    rows = sum(9 * n + 16 for _, _, n in takes)
    return pl.pallas_call(
        functools.partial(widen_kernel, takes),
        in_specs=[smem(), smem()] + whole(5),
        out_specs=whole(1)[0],
        out_shape=jax.ShapeDtypeStruct((rows, LANES), kind),
        compiler_params=params(16),
        cost_estimate=cost(200_000_000, 6_000_000),
        name="widen",
    )(core, z, part, own, other, gate, upper)


BLOCK = 592
TO_LOWER = ((7, 0, 64), (2, 0, 64), (4, 0, 32))
TO_UPPER = ((1, 0, 64), (6, 0, 64), (4, 32, 32))
TO_KEEP = ((0, 0, 64), (5, 0, 64), (3, 0, 64))


def merge_kernel(keep_ref, above_ref, below_ref, stay_ref, down_ref, up_ref):
    def block(ref, k):
        return ref[k * BLOCK : (k + 1) * BLOCK].astype(F32)

    stay_ref[...] = block(keep_ref, 0) + block(above_ref, 0) + block(below_ref, 0)
    for out_ref, k, full_ref, half_ref, shift in (
        (down_ref, 1, below_ref, above_ref, 0),
        (up_ref, 2, above_ref, below_ref, 32),
    ):
        total = block(keep_ref, k) + block(full_ref, 1)
        half = half_ref[2 * BLOCK :].astype(F32)
        for j in range(9):
            at = j * 64
            out_ref[at + 32 - shift : at + 64 - shift] = total[
                at + 32 - shift : at + 64 - shift
            ].astype(BF16)
            value = total[at + shift : at + shift + 32] + half[j * 32 : (j + 1) * 32]
            out_ref[at + shift : at + shift + 32] = value.astype(BF16)
        line = jnp.sum(total[576:592] + half[288:304], axis=0, keepdims=True)
        out_ref[576:592] = tile_of(line, False).astype(BF16)


def merge(keep, above, below):
    shapes = [jax.ShapeDtypeStruct((BLOCK, LANES), kind) for kind in (F32, BF16, BF16)]
    return pl.pallas_call(
        merge_kernel,
        in_specs=whole(3),
        out_specs=whole(3),
        out_shape=shapes,
        compiler_params=params(16),
        cost_estimate=cost(5_000_000, 3_000_000),
        name="merge",
    )(keep, above, below)


def gated(gate, upper):
    return gate / (1.0 + jnp.exp(-gate)) * upper


def hidden_kernel(stay_ref, above_ref, below_ref, out_ref):
    chunk = 64

    def total(at, rows):
        value = above_ref[at : at + rows].astype(F32) + below_ref[at : at + rows].astype(F32)
        return stay_ref[at : at + rows] + value

    line = jnp.sum(total(576, 16), axis=0, keepdims=True)
    same = iota((chunk, LANES), 0) == iota((chunk, LANES), 1)
    squares = jnp.sum(jnp.where(same, line, 0.0), axis=1, keepdims=True)
    rstd = lax.rsqrt(squares / D + 1e-06)

    def put(at, value):
        out_ref[at : at + value.shape[0]] = value.astype(BF16)

    for j in range(4):
        gate = total(j * chunk, chunk) * rstd
        put(j * chunk, gated(gate, total((4 + j) * chunk, chunk) * rstd))
    mixed = total(8 * chunk, chunk) * rstd
    value = gated(mixed, pltpu.roll(mixed, 64, 1))
    lane = iota((32, LANES), 1)
    put(256, jnp.where(lane < 64, value[:32], pltpu.roll(value[32:], 64, 1)))


def make_hidden(stay, above, below):
    return pl.pallas_call(
        hidden_kernel,
        in_specs=whole(3),
        out_specs=whole(1)[0],
        out_shape=jax.ShapeDtypeStruct((288, LANES), BF16),
        compiler_params=params(16),
        cost_estimate=cost(5_000_000, 2_000_000),
        name="hidden",
    )(stay, above, below)


def down_kernel(turn, core_ref, z_ref, units_ref, w_ref, *rest):
    core = core_ref[0] if turn == 0 else 1 - core_ref[0]
    low = core == 0
    rows = pl.ds(pl.multiple_of(core * 640, LANES), 512)
    blocks = [units_ref[:, j * 64 : (j + 1) * 64].reshape(512, LANES) for j in range(4)]
    total = dot(jnp.concatenate(blocks, axis=1), w_ref[:, rows], ((1,), (1,)))
    packed = units_ref[:, 256:288].astype(F32).reshape(256, LANES)
    turned = pltpu.roll(packed, 64, 1)
    lane = iota(packed.shape, 1)
    begin = jnp.where(low, 0, 64)
    here = (lane >= begin) & (lane < begin + 64)
    top = jnp.where(here, jnp.where(low, packed, turned), 0.0).reshape(8, 32, LANES)
    bottom = jnp.where(here, jnp.where(low, turned, packed), 0.0).reshape(8, 32, LANES)
    mixed = jnp.concatenate([top, bottom], axis=1).reshape(512, LANES).astype(BF16)
    total = total + dot(mixed, w_ref[:, 512:640], ((1,), (1,)))
    if turn == 1:
        place_chunks(rest[1], z_ref[0], total + rest[0][...])
    else:
        rest[0][...] = total


def down(core, z, units, w_down, before=None):
    turn = 0 if before is None else 1
    return pl.pallas_call(
        functools.partial(down_kernel, turn),
        in_specs=[smem(), smem()] + whole(2 + turn),
        out_specs=whole(1)[0],
        out_shape=jax.ShapeDtypeStruct((512, w_down.shape[0]), BF16 if turn else F32),
        compiler_params=params(16),
        cost_estimate=cost(280_000_000, 2_000_000),
        name="down" + "ab"[turn],
    )(core, z, units, w_down, *([before] if turn else []))


def last_kernel(parts_ref, mid_ref, out_ref):
    total = parts_ref[0].astype(F32)
    for k in range(1, parts_ref.shape[0]):
        total = total + parts_ref[k].astype(F32)
    out_ref[...] = (mid_ref[...].astype(F32) + total).astype(BF16)


def last(parts, mid):
    return pl.pallas_call(
        last_kernel,
        in_specs=whole(2),
        out_specs=whole(1)[0],
        out_shape=jax.ShapeDtypeStruct(mid.shape, BF16),
        compiler_params=params(16),
        cost_estimate=cost(1_000_000, 1_000_000),
        name="last",
    )(parts, mid)


def exchange(x, axes):
    return lax.all_to_all(x, axes, split_axis=0, concat_axis=0, tiled=True)


def swap(x):
    return lax.ppermute(x, "core", [(0, 1), (1, 0)])


def shift(x, far):
    return lax.ppermute(x, "z", [(i, (i + far) % 8) for i in range(8)])


def gather(x):
    one_above, one_below = shift(x, 7), shift(x, 1)
    two_above, two_below = shift(x, 6), shift(x, 2)
    three_above, three_below = shift(two_above, 7), shift(two_below, 1)
    opposite = shift(two_above, 6)
    return pack(
        [x, one_above, one_below, two_above, two_below, three_above, three_below, opposite]
    )


def body(
    q_latent,
    q_rope,
    latent_cache,
    rope_cache,
    indices,
    w_uv,
    w_out,
    residual,
    norm_gain,
    w_gate,
    w_up,
    w_down,
):
    core = lax.axis_index("core").astype(jnp.int32).reshape(1)
    place = lax.axis_index(HID).astype(jnp.int32).reshape(1)
    height = lax.axis_index("z").astype(jnp.int32).reshape(1)
    gate_other = swap(w_gate)
    up_other = swap(w_up)

    context = attend(indices, q_latent, q_rope, latent_cache, rope_cache)
    moved = exchange(context.reshape(32, 8, LAT), LAYER).reshape(256, LAT)
    flat = gather(heads(core, moved, w_uv))
    other = swap(flat)
    part = project(core, height, flat, w_out.T)
    partial = project(core, height, other, w_out.T, part)
    parts = exchange(partial.reshape(16, 32, -1), HID)
    mid, scaled = middle(place, parts, residual, norm_gain[None, :])
    scaled = exchange(scaled, HID).reshape(512, 512)
    scaled_other = swap(scaled)
    part = first(core, scaled, w_gate, w_up)
    rest = (core, height, part, scaled, scaled_other, gate_other, up_other)
    from_above = shift(widen(TO_LOWER, BF16, *rest), 7)
    from_below = shift(widen(TO_UPPER, BF16, *rest), 1)
    stay, lower, upper = merge(widen(TO_KEEP, F32, *rest), from_above, from_below)
    hidden = gather(make_hidden(stay, shift(lower, 5), shift(upper, 3)))
    other = swap(hidden).reshape(8, 288, LANES)
    part = down(core, height, hidden.reshape(8, 288, LANES), w_down.T)
    outer = down(core, height, other, w_down.T, part)
    return last(exchange(outer.reshape(16, 32, -1), HID), mid)


def solution(mesh):
    axes = Mesh(mesh.devices.reshape(8, 2, 4, 4), ("z", "core", "y", "x"))
    rows = ("z", "core")
    every = ("z", "core", "y", "x")
    placed = (
        P(every, None, None),
        P(every, None, None),
        P(every, None, None),
        P(every, None, None),
        P(every, None),
        P(HID, None, None),
        P(HID, rows),
        P(None, rows),
        P(rows),
        P(rows, HID),
        P(rows, HID),
        P(HID, rows),
    )
    return jax.shard_map(
        body, mesh=axes, in_specs=placed, out_specs=P(HID, rows), check_vma=False
    )
```

```python
import functools
import math

import jax
import jax.numpy as jnp
from jax import lax
from jax.experimental import pallas as pl
from jax.experimental.pallas import tpu as pltpu
from jax.sharding import Mesh
from jax.sharding import PartitionSpec as P

D = 7168
ROPE = 64
VDIM = 128
LAT = 512
HEADS = 128
CTX = 3072
F32 = jnp.float32
BF16 = jnp.bfloat16
HID = ("y", "x")
LAYER = ("core", "y", "x")
LANES = 128
FAR = (0, 1, 7, 2, 6, 3, 5, 4)
EXP2_SCALE = math.log2(math.e) / math.sqrt(VDIM + ROPE)


def dot(a, b, dims=((1,), (0,))):
    return lax.dot_general(a, b, (dims, ((), ())), preferred_element_type=F32)


def iota(shape, dim):
    return lax.broadcasted_iota(jnp.int32, shape, dim)


def whole(n):
    return [pl.BlockSpec(memory_space=pltpu.VMEM)] * n


def smem():
    return pl.BlockSpec(memory_space=pltpu.SMEM)


def params(mib):
    return pltpu.CompilerParams(vmem_limit_bytes=mib * 2**20)


def cost(flops, nbytes):
    return pl.CostEstimate(flops=flops, bytes_accessed=nbytes, transcendentals=0)


def attend_kernel(idx_ref, ql_ref, qr_ref, lat_ref, rope_ref, out_ref, scores, both):
    seq = pl.program_id(0)
    idx = idx_ref[pl.ds(seq, 1), :]
    high = (iota((32, idx.shape[1]), 0) == lax.shift_right_logical(idx, 7)).astype(F32).astype(BF16)
    low = (iota((LANES, idx.shape[1]), 0) == (idx & 127)).astype(F32).astype(BF16)
    bias = jnp.where(dot(low, high, ((1,), (1,))) > 0.5, 0.0, -1e30)

    q_lat = ql_ref[0]
    q_rope = qr_ref[0]
    step = 1024
    top = jnp.full((8, HEADS), -3e38, F32)
    for at in range(0, CTX, step):
        part = dot(lat_ref[0, at : at + step, :], q_lat, ((1,), (1,)))
        part = part + dot(rope_ref[0, :, at : at + step], q_rope, ((0,), (0,)))
        for j in range(step // LANES):
            g = at // LANES + j
            piece = part[j * LANES : (j + 1) * LANES] + bias[:, g : g + 1]
            scores[g * LANES : (g + 1) * LANES, :] = piece
            top = jnp.maximum(top, jnp.max(piece.reshape(16, 8, HEADS), axis=0))
    peak = jnp.max(top, axis=0, keepdims=True)
    total = jnp.zeros((8, HEADS), F32)
    acc = jnp.zeros((HEADS, LAT), F32)
    for at in range(0, CTX, step):
        e = jnp.exp2((scores[at : at + step, :] - peak) * EXP2_SCALE)
        total = total + jnp.sum(e.reshape(step // 8, 8, HEADS), axis=0)
        acc = acc + dot(e.astype(BF16), lat_ref[0, at : at + step, :], ((0,), (0,)))
    norm = jnp.sum(total, axis=0, keepdims=True)
    same = iota((HEADS, HEADS), 0) == iota((HEADS, HEADS), 1)
    norm = jnp.sum(jnp.where(same, norm, 0.0), axis=1, keepdims=True)
    both[pl.ds(pl.multiple_of(seq * HEADS, HEADS), HEADS), :] = (acc / norm).astype(BF16)

    @pl.when(seq == 1)
    def _():
        row = iota((256, 256), 0)
        col = iota((256, 256), 1)
        i, s, h, c = row & 3, (row >> 2) & 1, (row >> 3) & 15, row >> 7
        pick = (col == s * HEADS + h * 8 + c * 4 + i).astype(F32).astype(BF16)
        out_ref[...] = dot(pick, both[...]).astype(BF16)


def attend(idx, q_lat, q_rope, lat, rope):
    return pl.pallas_call(
        attend_kernel,
        grid=(2,),
        in_specs=[
            pl.BlockSpec(idx.shape, lambda s: (0, 0)),
            pl.BlockSpec((1, HEADS, LAT), lambda s: (s, 0, 0)),
            pl.BlockSpec((1, ROPE, HEADS), lambda s: (s, 0, 0)),
            pl.BlockSpec((1, CTX, LAT), lambda s: (s, 0, 0)),
            pl.BlockSpec((1, ROPE, CTX), lambda s: (s, 0, 0)),
        ],
        out_specs=pl.BlockSpec((256, LAT), lambda s: (0, 0)),
        out_shape=jax.ShapeDtypeStruct((256, LAT), BF16),
        scratch_shapes=[pltpu.VMEM((CTX, HEADS), F32), pltpu.VMEM((256, LAT), BF16)],
        compiler_params=params(58),
        cost_estimate=cost(1_800_000_000, 8_000_000),
        name="attend",
    )(idx, q_lat, q_rope, lat, rope)


def heads_kernel(core_ref, x_ref, w_ref, out_ref):
    core = core_ref[0]
    row = iota((256, 256), 0)
    col = iota((256, 256), 1)
    pick = (col == (row & 63) * 4 + (row >> 6)).astype(F32).astype(BF16)
    sorted_rows = dot(pick, x_ref[...]).astype(BF16)
    for i in range(4):
        part = dot(sorted_rows[i * 64 : (i + 1) * 64], w_ref[core * 4 + i]).astype(BF16)
        out_ref[:, i * VDIM : (i + 1) * VDIM] = part


def heads(core, x, w_uv):
    return pl.pallas_call(
        heads_kernel,
        in_specs=[smem()] + whole(2),
        out_specs=whole(1)[0],
        out_shape=jax.ShapeDtypeStruct((64, 512), BF16),
        compiler_params=params(16),
        cost_estimate=cost(100_000_000, 2_000_000),
        name="heads",
    )(core, x, w_uv)


def pack_kernel(*refs):
    rows = refs[0].shape[0]
    for k, ref in enumerate(refs[:-1]):
        refs[-1][k * rows : (k + 1) * rows] = ref[...]


def pack(blocks):
    rows, columns = blocks[0].shape
    return pl.pallas_call(
        pack_kernel,
        in_specs=whole(8),
        out_specs=whole(1)[0],
        out_shape=jax.ShapeDtypeStruct((8 * rows, columns), BF16),
        compiler_params=params(16),
        cost_estimate=cost(0, 1_000_000),
        name="pack",
    )(*blocks)


def place_chunks(out_ref, z, value):
    for k, far in enumerate(FAR):
        at = pl.multiple_of(lax.rem(z + far, 8) * 64, 64)
        out_ref[pl.ds(at, 64), :] = value[k * 64 : (k + 1) * 64].astype(out_ref.dtype)


def project_kernel(turn, core_ref, z_ref, heads_ref, w_ref, *rest):
    half = core_ref[0] if turn == 0 else 1 - core_ref[0]
    rows = pl.ds(pl.multiple_of(half * 512, 512), 512)
    total = dot(heads_ref[...], w_ref[:, rows], ((1,), (1,)))
    if turn == 1:
        place_chunks(rest[1], z_ref[0], total + rest[0][...])
    else:
        rest[0][...] = total


def project(core, z, own, w_out, before=None):
    turn = 0 if before is None else 1
    return pl.pallas_call(
        functools.partial(project_kernel, turn),
        in_specs=[smem(), smem()] + whole(2 + turn),
        out_specs=whole(1)[0],
        out_shape=jax.ShapeDtypeStruct((512, w_out.shape[0]), BF16 if turn else F32),
        compiler_params=params(16),
        cost_estimate=cost(240_000_000, 2_000_000),
        name="project" + "ab"[turn],
    )(core, z, own, w_out, *([before] if turn else []))


def middle_kernel(place_ref, parts_ref, res_ref, gain_ref, mid_ref, out_ref):
    rows, cols = mid_ref.shape
    total = parts_ref[0].astype(F32)
    for k in range(1, parts_ref.shape[0]):
        total = total + parts_ref[k].astype(F32)
    res = res_ref[pl.ds(pl.multiple_of(place_ref[0] * rows, rows), rows), :]
    mid = (res.astype(F32) + total).astype(BF16)
    mid_ref[...] = mid
    wide = mid.astype(F32)
    squares = jnp.sum(wide * wide, axis=1, keepdims=True)
    upper = squares.astype(BF16).astype(F32)
    lane = iota((rows, 512 - cols), 1)
    extra = jnp.where(lane == 0, upper, jnp.where(lane == 1, squares - upper, 0.0)).astype(BF16)
    scaled = (wide * gain_ref[...].astype(F32)).astype(BF16)
    for k in range(out_ref.shape[0]):
        out_ref[k, :, :cols] = scaled
        out_ref[k, :, cols:] = extra


def middle(place, parts, residual, gain):
    rows, cols = parts.shape[1:]
    return pl.pallas_call(
        middle_kernel,
        in_specs=[smem()] + whole(3),
        out_specs=whole(2),
        out_shape=[
            jax.ShapeDtypeStruct((rows, cols), BF16),
            jax.ShapeDtypeStruct((16, rows, 512), BF16),
        ],
        compiler_params=params(16),
        cost_estimate=cost(2_500_000_000, 1_500_000),
        name="middle",
    )(place, parts, residual, gain)


def first_kernel(core_ref, own_ref, g_ref, u_ref, out_ref):
    deep = g_ref.shape[0]
    full = pl.ds(pl.multiple_of(core_ref[0] * 640, LANES), 512)
    own = own_ref[:, :deep]
    out_ref[:, 0:512] = dot(own, g_ref[:, full])
    out_ref[:, 512:1024] = dot(own, u_ref[:, full])
    out_ref[:, 1024:1152] = dot(own, g_ref[:, 512:640])
    out_ref[:, 1152:1280] = dot(own, u_ref[:, 512:640])


def first(core, own, gate, upper):
    return pl.pallas_call(
        first_kernel,
        in_specs=[smem()] + whole(3),
        out_specs=whole(1)[0],
        out_shape=jax.ShapeDtypeStruct((512, 1280), F32),
        compiler_params=params(16),
        cost_estimate=cost(560_000_000, 5_000_000),
        name="first",
    )(core, own, gate, upper)


def widen_kernel(lists, core_ref, z_ref, part_ref, own_ref, other_ref, g_ref, u_ref, *outs):
    deep = g_ref.shape[0]
    low = core_ref[0] == 0
    full = pl.ds(pl.multiple_of(core_ref[0] * 640, LANES), 512)
    wide = outs[0].dtype == F32
    places = []
    source = 0
    for out_ref, takes in zip(outs, lists):
        at = 0
        for far, begin, rows in takes:
            places.append((out_ref, at, source, far, begin, rows))
            at += 9 * rows + 16
            source += rows

    def rows_of(ref, columns):
        pieces = []
        for _, _, _, far, begin, rows in places:
            at = lax.rem(z_ref[0] + far, 8) * 64 + begin
            pieces.append(ref[pl.ds(pl.multiple_of(at, 32), rows), columns])
        return jnp.concatenate(pieces, axis=0)

    other = rows_of(other_ref, slice(0, deep))

    def put(block, value):
        value = value.astype(outs[0].dtype)
        for out_ref, at, source, _, _, rows in places:
            for j in range(value.shape[1] // LANES):
                begin = at + (block + j) * rows
                out_ref[begin : begin + rows] = value[
                    source : source + rows, j * LANES : (j + 1) * LANES
                ]

    put(0, rows_of(part_ref, slice(0, 512)) + dot(other, g_ref[:, full]))
    put(4, rows_of(part_ref, slice(512, 1024)) + dot(other, u_ref[:, full]))
    gate = rows_of(part_ref, slice(1024, 1152)) + dot(other, g_ref[:, 512:640])
    upper = rows_of(part_ref, slice(1152, 1280)) + dot(other, u_ref[:, 512:640])
    straight = jnp.where(low, gate, upper)
    turned = pltpu.roll(jnp.where(low, upper, gate), 64, 1)
    lane = iota(gate.shape, 1)
    begin = jnp.where(low, 0, 64)
    put(8, jnp.where((lane >= begin) & (lane < begin + 64), straight, turned))
    extra = slice(deep, 512)
    squares = jnp.sum(rows_of(own_ref, extra).astype(F32), axis=1, keepdims=True)
    squares = squares + jnp.sum(rows_of(other_ref, extra).astype(F32), axis=1, keepdims=True)
    for out_ref, at, source, _, first_row, rows in places:
        same = iota((rows, LANES), 0) + first_row == iota((rows, LANES), 1)
        line = jnp.where(same, squares[source : source + rows], 0.0)
        line = jnp.sum(line, axis=0, keepdims=True)
        out_ref[at + 9 * rows : at + 9 * rows + 16] = tile_of(line, wide).astype(out_ref.dtype)


def tile_of(line, wide):
    row = iota((16, LANES), 0)
    high = line if wide else line.astype(BF16).astype(F32)
    return jnp.where(row == 0, high, jnp.where(row == 1, line - high, 0.0))


def widen(lists, kind, core, z, part, own, other, gate, upper):
    shapes = [
        jax.ShapeDtypeStruct((sum(9 * n + 16 for _, _, n in takes), LANES), kind) for takes in lists
    ]
    return pl.pallas_call(
        functools.partial(widen_kernel, lists),
        in_specs=[smem(), smem()] + whole(5),
        out_specs=whole(len(lists)),
        out_shape=shapes,
        compiler_params=params(16),
        cost_estimate=cost(200_000_000, 6_000_000),
        name="widen",
    )(core, z, part, own, other, gate, upper)


BLOCK = 592
TO_LOWER = ((7, 0, 64), (5, 0, 64))
TO_UPPER = ((1, 0, 64), (3, 0, 64))
TWO_LOWER = ((4, 0, 32),)
TWO_UPPER = ((4, 32, 32),)
TO_KEEP = ((0, 0, 64), (6, 0, 64), (2, 0, 64))


def merge_kernel(keep_ref, above_ref, below_ref, far_above_ref, far_below_ref, stay_ref, down_ref, up_ref):
    def block(ref, k):
        return ref[k * BLOCK : (k + 1) * BLOCK].astype(F32)

    stay_ref[...] = block(keep_ref, 0) + block(above_ref, 0) + block(below_ref, 0)
    for out_ref, k, full_ref, half_ref, shift in (
        (down_ref, 1, above_ref, far_above_ref, 0),
        (up_ref, 2, below_ref, far_below_ref, 32),
    ):
        total = block(keep_ref, k) + block(full_ref, 1)
        half = half_ref[...].astype(F32)
        for j in range(9):
            at = j * 64
            out_ref[at + 32 - shift : at + 64 - shift] = total[
                at + 32 - shift : at + 64 - shift
            ].astype(BF16)
            value = total[at + shift : at + shift + 32] + half[j * 32 : (j + 1) * 32]
            out_ref[at + shift : at + shift + 32] = value.astype(BF16)
        line = jnp.sum(total[576:592] + half[288:304], axis=0, keepdims=True)
        out_ref[576:592] = tile_of(line, False).astype(BF16)


def merge(*parts):
    shapes = [jax.ShapeDtypeStruct((BLOCK, LANES), kind) for kind in (F32, BF16, BF16)]
    return pl.pallas_call(
        merge_kernel,
        in_specs=whole(5),
        out_specs=whole(3),
        out_shape=shapes,
        compiler_params=params(16),
        cost_estimate=cost(5_000_000, 3_000_000),
        name="merge",
    )(*parts)


def gated(gate, upper):
    return gate / (1.0 + jnp.exp(-gate)) * upper


def hidden_kernel(stay_ref, above_ref, below_ref, out_ref):
    chunk = 64

    def total(at, rows):
        value = above_ref[at : at + rows].astype(F32) + below_ref[at : at + rows].astype(F32)
        return stay_ref[at : at + rows] + value

    line = jnp.sum(total(576, 16), axis=0, keepdims=True)
    same = iota((chunk, LANES), 0) == iota((chunk, LANES), 1)
    squares = jnp.sum(jnp.where(same, line, 0.0), axis=1, keepdims=True)
    rstd = lax.rsqrt(squares / D + 1e-06)

    def put(at, value):
        out_ref[at : at + value.shape[0]] = value.astype(BF16)

    for j in range(4):
        gate = total(j * chunk, chunk) * rstd
        put(j * chunk, gated(gate, total((4 + j) * chunk, chunk) * rstd))
    mixed = total(8 * chunk, chunk) * rstd
    value = gated(mixed, pltpu.roll(mixed, 64, 1))
    lane = iota((32, LANES), 1)
    put(256, jnp.where(lane < 64, value[:32], pltpu.roll(value[32:], 64, 1)))


def make_hidden(stay, above, below):
    return pl.pallas_call(
        hidden_kernel,
        in_specs=whole(3),
        out_specs=whole(1)[0],
        out_shape=jax.ShapeDtypeStruct((288, LANES), BF16),
        compiler_params=params(16),
        cost_estimate=cost(5_000_000, 2_000_000),
        name="hidden",
    )(stay, above, below)


def down_kernel(turn, core_ref, z_ref, units_ref, w_ref, *rest):
    core = core_ref[0] if turn == 0 else 1 - core_ref[0]
    low = core == 0
    rows = pl.ds(pl.multiple_of(core * 640, LANES), 512)
    blocks = [units_ref[:, j * 64 : (j + 1) * 64].reshape(512, LANES) for j in range(4)]
    total = dot(jnp.concatenate(blocks, axis=1), w_ref[:, rows], ((1,), (1,)))
    packed = units_ref[:, 256:288].astype(F32).reshape(256, LANES)
    turned = pltpu.roll(packed, 64, 1)
    lane = iota(packed.shape, 1)
    begin = jnp.where(low, 0, 64)
    here = (lane >= begin) & (lane < begin + 64)
    top = jnp.where(here, jnp.where(low, packed, turned), 0.0).reshape(8, 32, LANES)
    bottom = jnp.where(here, jnp.where(low, turned, packed), 0.0).reshape(8, 32, LANES)
    mixed = jnp.concatenate([top, bottom], axis=1).reshape(512, LANES).astype(BF16)
    total = total + dot(mixed, w_ref[:, 512:640], ((1,), (1,)))
    if turn == 1:
        place_chunks(rest[1], z_ref[0], total + rest[0][...])
    else:
        rest[0][...] = total


def down(core, z, units, w_down, before=None):
    turn = 0 if before is None else 1
    return pl.pallas_call(
        functools.partial(down_kernel, turn),
        in_specs=[smem(), smem()] + whole(2 + turn),
        out_specs=whole(1)[0],
        out_shape=jax.ShapeDtypeStruct((512, w_down.shape[0]), BF16 if turn else F32),
        compiler_params=params(16),
        cost_estimate=cost(280_000_000, 2_000_000),
        name="down" + "ab"[turn],
    )(core, z, units, w_down, *([before] if turn else []))


def last_kernel(parts_ref, mid_ref, out_ref):
    total = parts_ref[0].astype(F32)
    for k in range(1, parts_ref.shape[0]):
        total = total + parts_ref[k].astype(F32)
    out_ref[...] = (mid_ref[...].astype(F32) + total).astype(BF16)


def last(parts, mid):
    return pl.pallas_call(
        last_kernel,
        in_specs=whole(2),
        out_specs=whole(1)[0],
        out_shape=jax.ShapeDtypeStruct(mid.shape, BF16),
        compiler_params=params(16),
        cost_estimate=cost(1_000_000, 1_000_000),
        name="last",
    )(parts, mid)


def exchange(x, axes):
    return lax.all_to_all(x, axes, split_axis=0, concat_axis=0, tiled=True)


def swap(x):
    return lax.ppermute(x, "core", [(0, 1), (1, 0)])


def shift(x, far):
    return lax.ppermute(x, "z", [(i, (i + far) % 8) for i in range(8)])


def gather(x):
    one_above, one_below = shift(x, 7), shift(x, 1)
    two_above, two_below = shift(x, 6), shift(x, 2)
    three_above, three_below = shift(two_above, 7), shift(two_below, 1)
    opposite = shift(two_above, 6)
    return pack(
        [x, one_above, one_below, two_above, two_below, three_above, three_below, opposite]
    )


def body(
    q_latent,
    q_rope,
    latent_cache,
    rope_cache,
    indices,
    w_uv,
    w_out,
    residual,
    norm_gain,
    w_gate,
    w_up,
    w_down,
):
    core = lax.axis_index("core").astype(jnp.int32).reshape(1)
    place = lax.axis_index(HID).astype(jnp.int32).reshape(1)
    height = lax.axis_index("z").astype(jnp.int32).reshape(1)
    gate_other = swap(w_gate)
    up_other = swap(w_up)

    context = attend(indices, q_latent, q_rope, latent_cache, rope_cache)
    moved = exchange(context.reshape(32, 8, LAT), LAYER).reshape(256, LAT)
    flat = gather(heads(core, moved, w_uv))
    other = swap(flat)
    part = project(core, height, flat, w_out.T)
    partial = project(core, height, other, w_out.T, part)
    parts = exchange(partial.reshape(16, 32, -1), HID)
    mid, scaled = middle(place, parts, residual, norm_gain[None, :])
    scaled = exchange(scaled, HID).reshape(512, 512)
    scaled_other = swap(scaled)
    part = first(core, scaled, w_gate, w_up)
    rest = (core, height, part, scaled, scaled_other, gate_other, up_other)
    two_lower, two_upper, lower, upper = widen((TWO_LOWER, TWO_UPPER, TO_LOWER, TO_UPPER), BF16, *rest)
    arrived = (shift(lower, 7), shift(upper, 1), shift(two_lower, 6), shift(two_upper, 2))
    (keep,) = widen((TO_KEEP,), F32, *rest)
    stay, lower, upper = merge(keep, *arrived)
    hidden = gather(make_hidden(stay, shift(lower, 6), shift(upper, 2)))
    other = swap(hidden).reshape(8, 288, LANES)
    part = down(core, height, hidden.reshape(8, 288, LANES), w_down.T)
    outer = down(core, height, other, w_down.T, part)
    return last(exchange(outer.reshape(16, 32, -1), HID), mid)


def solution(mesh):
    axes = Mesh(mesh.devices.reshape(8, 2, 4, 4), ("z", "core", "y", "x"))
    rows = ("z", "core")
    every = ("z", "core", "y", "x")
    placed = (
        P(every, None, None),
        P(every, None, None),
        P(every, None, None),
        P(every, None, None),
        P(every, None),
        P(HID, None, None),
        P(HID, rows),
        P(None, rows),
        P(rows),
        P(rows, HID),
        P(rows, HID),
        P(HID, rows),
    )
    return jax.shard_map(
        body, mesh=axes, in_specs=placed, out_specs=P(HID, rows), check_vma=False
    )
```

```python
import functools
import math

import jax
import jax.numpy as jnp
from jax import lax
from jax.experimental import pallas as pl
from jax.experimental.pallas import tpu as pltpu
from jax.sharding import Mesh
from jax.sharding import PartitionSpec as P

D = 7168
ROPE = 64
VDIM = 128
LAT = 512
HEADS = 128
CTX = 3072
F32 = jnp.float32
BF16 = jnp.bfloat16
HID = ("y", "x")
LAYER = ("core", "y", "x")
LANES = 128
FAR = (0, 1, 7, 2, 6, 3, 5, 4)
EXP2_SCALE = math.log2(math.e) / math.sqrt(VDIM + ROPE)


def dot(a, b, dims=((1,), (0,))):
    return lax.dot_general(a, b, (dims, ((), ())), preferred_element_type=F32)


def iota(shape, dim):
    return lax.broadcasted_iota(jnp.int32, shape, dim)


def whole(n):
    return [pl.BlockSpec(memory_space=pltpu.VMEM)] * n


def smem():
    return pl.BlockSpec(memory_space=pltpu.SMEM)


def params(mib):
    return pltpu.CompilerParams(vmem_limit_bytes=mib * 2**20)


def cost(flops, nbytes):
    return pl.CostEstimate(flops=flops, bytes_accessed=nbytes, transcendentals=0)


def attend_kernel(idx_ref, ql_ref, qr_ref, lat_ref, rope_ref, out_ref, scores, both):
    seq = pl.program_id(0)
    idx = idx_ref[pl.ds(seq, 1), :]
    high = (iota((32, idx.shape[1]), 0) == lax.shift_right_logical(idx, 7)).astype(F32).astype(BF16)
    low = (iota((LANES, idx.shape[1]), 0) == (idx & 127)).astype(F32).astype(BF16)
    bias = jnp.where(dot(low, high, ((1,), (1,))) > 0.5, 0.0, -1e30)

    q_lat = ql_ref[0]
    q_rope = qr_ref[0]
    step = 1024
    top = jnp.full((8, HEADS), -3e38, F32)
    for at in range(0, CTX, step):
        part = dot(lat_ref[0, at : at + step, :], q_lat, ((1,), (1,)))
        part = part + dot(rope_ref[0, :, at : at + step], q_rope, ((0,), (0,)))
        for j in range(step // LANES):
            g = at // LANES + j
            piece = part[j * LANES : (j + 1) * LANES] + bias[:, g : g + 1]
            scores[g * LANES : (g + 1) * LANES, :] = piece
            top = jnp.maximum(top, jnp.max(piece.reshape(16, 8, HEADS), axis=0))
    peak = jnp.max(top, axis=0, keepdims=True)
    total = jnp.zeros((8, HEADS), F32)
    acc = jnp.zeros((HEADS, LAT), F32)
    for at in range(0, CTX, step):
        e = jnp.exp2((scores[at : at + step, :] - peak) * EXP2_SCALE)
        total = total + jnp.sum(e.reshape(step // 8, 8, HEADS), axis=0)
        acc = acc + dot(e.astype(BF16), lat_ref[0, at : at + step, :], ((0,), (0,)))
    norm = jnp.sum(total, axis=0, keepdims=True)
    same = iota((HEADS, HEADS), 0) == iota((HEADS, HEADS), 1)
    norm = jnp.sum(jnp.where(same, norm, 0.0), axis=1, keepdims=True)
    both[pl.ds(pl.multiple_of(seq * HEADS, HEADS), HEADS), :] = (acc / norm).astype(BF16)

    @pl.when(seq == 1)
    def _():
        row = iota((256, 256), 0)
        col = iota((256, 256), 1)
        i, s, h, c = row & 3, (row >> 2) & 1, (row >> 3) & 15, row >> 7
        pick = (col == s * HEADS + h * 8 + c * 4 + i).astype(F32).astype(BF16)
        out_ref[...] = dot(pick, both[...]).astype(BF16)


def attend(idx, q_lat, q_rope, lat, rope):
    return pl.pallas_call(
        attend_kernel,
        grid=(2,),
        in_specs=[
            pl.BlockSpec(idx.shape, lambda s: (0, 0)),
            pl.BlockSpec((1, HEADS, LAT), lambda s: (s, 0, 0)),
            pl.BlockSpec((1, ROPE, HEADS), lambda s: (s, 0, 0)),
            pl.BlockSpec((1, CTX, LAT), lambda s: (s, 0, 0)),
            pl.BlockSpec((1, ROPE, CTX), lambda s: (s, 0, 0)),
        ],
        out_specs=pl.BlockSpec((256, LAT), lambda s: (0, 0)),
        out_shape=jax.ShapeDtypeStruct((256, LAT), BF16),
        scratch_shapes=[pltpu.VMEM((CTX, HEADS), F32), pltpu.VMEM((256, LAT), BF16)],
        compiler_params=params(58),
        cost_estimate=cost(1_800_000_000, 8_000_000),
        name="attend",
    )(idx, q_lat, q_rope, lat, rope)


def heads_kernel(core_ref, x_ref, w_ref, out_ref):
    core = core_ref[0]
    row = iota((256, 256), 0)
    col = iota((256, 256), 1)
    pick = (col == (row & 63) * 4 + (row >> 6)).astype(F32).astype(BF16)
    sorted_rows = dot(pick, x_ref[...]).astype(BF16)
    for i in range(4):
        part = dot(sorted_rows[i * 64 : (i + 1) * 64], w_ref[core * 4 + i]).astype(BF16)
        out_ref[:, i * VDIM : (i + 1) * VDIM] = part


def heads(core, x, w_uv):
    return pl.pallas_call(
        heads_kernel,
        in_specs=[smem()] + whole(2),
        out_specs=whole(1)[0],
        out_shape=jax.ShapeDtypeStruct((64, 512), BF16),
        compiler_params=params(16),
        cost_estimate=cost(100_000_000, 2_000_000),
        name="heads",
    )(core, x, w_uv)


def pack_kernel(*refs):
    rows = refs[0].shape[0]
    for k, ref in enumerate(refs[:-1]):
        refs[-1][k * rows : (k + 1) * rows] = ref[...]


def pack(blocks):
    rows, columns = blocks[0].shape
    return pl.pallas_call(
        pack_kernel,
        in_specs=whole(8),
        out_specs=whole(1)[0],
        out_shape=jax.ShapeDtypeStruct((8 * rows, columns), BF16),
        compiler_params=params(16),
        cost_estimate=cost(0, 1_000_000),
        name="pack",
    )(*blocks)


def place_chunks(out_ref, z, value):
    for k, far in enumerate(FAR):
        at = pl.multiple_of(lax.rem(z + far, 8) * 64, 64)
        out_ref[pl.ds(at, 64), :] = value[k * 64 : (k + 1) * 64].astype(out_ref.dtype)


def project_kernel(turn, core_ref, z_ref, heads_ref, w_ref, *rest):
    if turn == 0:
        place_ref, res_hbm, out_ref, mine_ref, res_ref, sem = rest
        count = mine_ref.shape[0]
        group = LANES // count
        lanes = pl.multiple_of(place_ref[0] // group * LANES, LANES)
        copy = pltpu.make_async_copy(res_hbm.at[:, pl.ds(lanes, LANES)], res_ref, sem)
        copy.start()
    half = core_ref[0] if turn == 0 else 1 - core_ref[0]
    rows = pl.ds(pl.multiple_of(half * 512, 512), 512)
    total = dot(heads_ref[...], w_ref[:, rows], ((1,), (1,)))
    if turn == 1:
        place_chunks(rest[1], z_ref[0], total + rest[0][...])
    else:
        out_ref[...] = total
        copy.wait()
        begin = lax.rem(place_ref[0], group) * count
        shape = (count, LANES)
        pick = (iota(shape, 1) == iota(shape, 0) + begin).astype(F32).astype(BF16)
        mine_ref[...] = dot(pick, res_ref[...], ((1,), (1,))).astype(BF16)


def project_first(core, z, own, w_out, place, residual):
    cols = w_out.shape[0]
    return pl.pallas_call(
        functools.partial(project_kernel, 0),
        in_specs=[smem(), smem()] + whole(2) + [smem(), pl.BlockSpec(memory_space=pltpu.HBM)],
        out_specs=whole(2),
        out_shape=[
            jax.ShapeDtypeStruct((512, cols), F32),
            jax.ShapeDtypeStruct((32, cols), BF16),
        ],
        scratch_shapes=[pltpu.VMEM((cols, LANES), BF16), pltpu.SemaphoreType.DMA],
        compiler_params=params(16),
        cost_estimate=cost(240_000_000, 2_000_000),
        name="projecta",
    )(core, z, own, w_out, place, residual)


def project(core, z, other, w_out, before):
    return pl.pallas_call(
        functools.partial(project_kernel, 1),
        in_specs=[smem(), smem()] + whole(3),
        out_specs=whole(1)[0],
        out_shape=jax.ShapeDtypeStruct((512, w_out.shape[0]), BF16),
        compiler_params=params(16),
        cost_estimate=cost(240_000_000, 2_000_000),
        name="projectb",
    )(core, z, other, w_out, before)


def middle_kernel(parts_ref, res_ref, gain_ref, mid_ref, out_ref):
    rows, cols = mid_ref.shape
    total = parts_ref[0].astype(F32)
    for k in range(1, parts_ref.shape[0]):
        total = total + parts_ref[k].astype(F32)
    mid = (res_ref[...].astype(F32) + total).astype(BF16)
    mid_ref[...] = mid
    wide = mid.astype(F32)
    squares = jnp.sum(wide * wide, axis=1, keepdims=True)
    upper = squares.astype(BF16).astype(F32)
    lane = iota((rows, 512 - cols), 1)
    extra = jnp.where(lane == 0, upper, jnp.where(lane == 1, squares - upper, 0.0)).astype(BF16)
    scaled = (wide * gain_ref[...].astype(F32)).astype(BF16)
    for k in range(out_ref.shape[0]):
        out_ref[k, :, :cols] = scaled
        out_ref[k, :, cols:] = extra


def middle(parts, residual, gain):
    rows, cols = parts.shape[1:]
    return pl.pallas_call(
        middle_kernel,
        in_specs=whole(3),
        out_specs=whole(2),
        out_shape=[
            jax.ShapeDtypeStruct((rows, cols), BF16),
            jax.ShapeDtypeStruct((16, rows, 512), BF16),
        ],
        compiler_params=params(16),
        cost_estimate=cost(2_500_000_000, 1_500_000),
        name="middle",
    )(parts, residual, gain)


def first_kernel(core_ref, own_ref, g_ref, u_ref, out_ref):
    deep = g_ref.shape[0]
    full = pl.ds(pl.multiple_of(core_ref[0] * 640, LANES), 512)
    own = own_ref[:, :deep]
    out_ref[:, 0:512] = dot(own, g_ref[:, full])
    out_ref[:, 512:1024] = dot(own, u_ref[:, full])
    out_ref[:, 1024:1152] = dot(own, g_ref[:, 512:640])
    out_ref[:, 1152:1280] = dot(own, u_ref[:, 512:640])


def first(core, own, gate, upper):
    return pl.pallas_call(
        first_kernel,
        in_specs=[smem()] + whole(3),
        out_specs=whole(1)[0],
        out_shape=jax.ShapeDtypeStruct((512, 1280), F32),
        compiler_params=params(16),
        cost_estimate=cost(560_000_000, 5_000_000),
        name="first",
    )(core, own, gate, upper)


def widen_kernel(lists, core_ref, z_ref, part_ref, own_ref, other_ref, g_ref, u_ref, *outs):
    deep = g_ref.shape[0]
    low = core_ref[0] == 0
    full = pl.ds(pl.multiple_of(core_ref[0] * 640, LANES), 512)
    wide = outs[0].dtype == F32
    places = []
    source = 0
    for out_ref, takes in zip(outs, lists):
        at = 0
        for far, begin, rows in takes:
            places.append((out_ref, at, source, far, begin, rows))
            at += 9 * rows + 16
            source += rows

    def rows_of(ref, columns):
        pieces = []
        for _, _, _, far, begin, rows in places:
            at = lax.rem(z_ref[0] + far, 8) * 64 + begin
            pieces.append(ref[pl.ds(pl.multiple_of(at, 32), rows), columns])
        return jnp.concatenate(pieces, axis=0)

    other = rows_of(other_ref, slice(0, deep))

    def put(block, value):
        value = value.astype(outs[0].dtype)
        for out_ref, at, source, _, _, rows in places:
            for j in range(value.shape[1] // LANES):
                begin = at + (block + j) * rows
                out_ref[begin : begin + rows] = value[
                    source : source + rows, j * LANES : (j + 1) * LANES
                ]

    put(0, rows_of(part_ref, slice(0, 512)) + dot(other, g_ref[:, full]))
    put(4, rows_of(part_ref, slice(512, 1024)) + dot(other, u_ref[:, full]))
    gate = rows_of(part_ref, slice(1024, 1152)) + dot(other, g_ref[:, 512:640])
    upper = rows_of(part_ref, slice(1152, 1280)) + dot(other, u_ref[:, 512:640])
    straight = jnp.where(low, gate, upper)
    turned = pltpu.roll(jnp.where(low, upper, gate), 64, 1)
    lane = iota(gate.shape, 1)
    begin = jnp.where(low, 0, 64)
    put(8, jnp.where((lane >= begin) & (lane < begin + 64), straight, turned))
    extra = slice(deep, 512)
    squares = jnp.sum(rows_of(own_ref, extra).astype(F32), axis=1, keepdims=True)
    squares = squares + jnp.sum(rows_of(other_ref, extra).astype(F32), axis=1, keepdims=True)
    for out_ref, at, source, _, first_row, rows in places:
        same = iota((rows, LANES), 0) + first_row == iota((rows, LANES), 1)
        line = jnp.where(same, squares[source : source + rows], 0.0)
        line = jnp.sum(line, axis=0, keepdims=True)
        out_ref[at + 9 * rows : at + 9 * rows + 16] = tile_of(line, wide).astype(out_ref.dtype)


def tile_of(line, wide):
    row = iota((16, LANES), 0)
    high = line if wide else line.astype(BF16).astype(F32)
    return jnp.where(row == 0, high, jnp.where(row == 1, line - high, 0.0))


def widen(lists, kind, core, z, part, own, other, gate, upper):
    shapes = [
        jax.ShapeDtypeStruct((sum(9 * n + 16 for _, _, n in takes), LANES), kind) for takes in lists
    ]
    return pl.pallas_call(
        functools.partial(widen_kernel, lists),
        in_specs=[smem(), smem()] + whole(5),
        out_specs=whole(len(lists)),
        out_shape=shapes,
        compiler_params=params(16),
        cost_estimate=cost(200_000_000, 6_000_000),
        name="widen",
    )(core, z, part, own, other, gate, upper)


BLOCK = 592
TO_LOWER = ((7, 0, 64), (5, 0, 64))
TO_UPPER = ((1, 0, 64), (3, 0, 64))
TO_OPPOSITE = ((4, 0, 64),)
TO_KEEP = ((0, 0, 64), (6, 0, 64), (2, 0, 64))


def merge_kernel(core_ref, keep_ref, above_ref, below_ref, far_ref, stay_ref, down_ref, up_ref):
    def block(ref, k):
        return ref[k * BLOCK : (k + 1) * BLOCK].astype(F32)

    stay_ref[...] = block(keep_ref, 0) + block(above_ref, 0) + block(below_ref, 0)
    far = far_ref[...].astype(F32)
    for out_ref, k, near_ref, goes in (
        (down_ref, 1, above_ref, core_ref[0] == 1),
        (up_ref, 2, below_ref, core_ref[0] == 0),
    ):
        total = block(keep_ref, k) + block(near_ref, 1) + jnp.where(goes, far, 0.0)
        out_ref[:576] = total[:576].astype(BF16)
        line = jnp.sum(total[576:], axis=0, keepdims=True)
        out_ref[576:] = tile_of(line, False).astype(BF16)


def merge(core, *parts):
    shapes = [jax.ShapeDtypeStruct((BLOCK, LANES), kind) for kind in (F32, BF16, BF16)]
    return pl.pallas_call(
        merge_kernel,
        in_specs=[smem()] + whole(4),
        out_specs=whole(3),
        out_shape=shapes,
        compiler_params=params(16),
        cost_estimate=cost(5_000_000, 3_000_000),
        name="merge",
    )(core, *parts)


def gated(gate, upper):
    return gate / (1.0 + jnp.exp(-gate)) * upper


def hidden_kernel(stay_ref, above_ref, below_ref, out_ref):
    chunk = 64

    def total(at, rows):
        value = above_ref[at : at + rows].astype(F32) + below_ref[at : at + rows].astype(F32)
        return stay_ref[at : at + rows] + value

    line = jnp.sum(total(576, 16), axis=0, keepdims=True)
    same = iota((chunk, LANES), 0) == iota((chunk, LANES), 1)
    squares = jnp.sum(jnp.where(same, line, 0.0), axis=1, keepdims=True)
    rstd = lax.rsqrt(squares / D + 1e-06)

    def put(at, value):
        out_ref[at : at + value.shape[0]] = value.astype(BF16)

    for j in range(4):
        gate = total(j * chunk, chunk) * rstd
        put(j * chunk, gated(gate, total((4 + j) * chunk, chunk) * rstd))
    mixed = total(8 * chunk, chunk) * rstd
    value = gated(mixed, pltpu.roll(mixed, 64, 1))
    lane = iota((32, LANES), 1)
    put(256, jnp.where(lane < 64, value[:32], pltpu.roll(value[32:], 64, 1)))


def make_hidden(stay, above, below):
    return pl.pallas_call(
        hidden_kernel,
        in_specs=whole(3),
        out_specs=whole(1)[0],
        out_shape=jax.ShapeDtypeStruct((288, LANES), BF16),
        compiler_params=params(16),
        cost_estimate=cost(5_000_000, 2_000_000),
        name="hidden",
    )(stay, above, below)


def down_kernel(turn, core_ref, z_ref, units_ref, w_ref, *rest):
    core = core_ref[0] if turn == 0 else 1 - core_ref[0]
    low = core == 0
    rows = pl.ds(pl.multiple_of(core * 640, LANES), 512)
    blocks = [units_ref[:, j * 64 : (j + 1) * 64].reshape(512, LANES) for j in range(4)]
    total = dot(jnp.concatenate(blocks, axis=1), w_ref[:, rows], ((1,), (1,)))
    packed = units_ref[:, 256:288].astype(F32).reshape(256, LANES)
    turned = pltpu.roll(packed, 64, 1)
    lane = iota(packed.shape, 1)
    begin = jnp.where(low, 0, 64)
    here = (lane >= begin) & (lane < begin + 64)
    top = jnp.where(here, jnp.where(low, packed, turned), 0.0).reshape(8, 32, LANES)
    bottom = jnp.where(here, jnp.where(low, turned, packed), 0.0).reshape(8, 32, LANES)
    mixed = jnp.concatenate([top, bottom], axis=1).reshape(512, LANES).astype(BF16)
    total = total + dot(mixed, w_ref[:, 512:640], ((1,), (1,)))
    if turn == 1:
        place_chunks(rest[1], z_ref[0], total + rest[0][...])
    else:
        rest[0][...] = total


def down(core, z, units, w_down, before=None):
    turn = 0 if before is None else 1
    return pl.pallas_call(
        functools.partial(down_kernel, turn),
        in_specs=[smem(), smem()] + whole(2 + turn),
        out_specs=whole(1)[0],
        out_shape=jax.ShapeDtypeStruct((512, w_down.shape[0]), BF16 if turn else F32),
        compiler_params=params(16),
        cost_estimate=cost(280_000_000, 2_000_000),
        name="down" + "ab"[turn],
    )(core, z, units, w_down, *([before] if turn else []))


def last_kernel(parts_ref, mid_ref, out_ref):
    total = parts_ref[0].astype(F32)
    for k in range(1, parts_ref.shape[0]):
        total = total + parts_ref[k].astype(F32)
    out_ref[...] = (mid_ref[...].astype(F32) + total).astype(BF16)


def last(parts, mid):
    return pl.pallas_call(
        last_kernel,
        in_specs=whole(2),
        out_specs=whole(1)[0],
        out_shape=jax.ShapeDtypeStruct(mid.shape, BF16),
        compiler_params=params(16),
        cost_estimate=cost(1_000_000, 1_000_000),
        name="last",
    )(parts, mid)


def exchange(x, axes):
    return lax.all_to_all(x, axes, split_axis=0, concat_axis=0, tiled=True)


def swap(x):
    return lax.ppermute(x, "core", [(0, 1), (1, 0)])


def shift(x, far):
    return lax.ppermute(x, "z", [(i, (i + far) % 8) for i in range(8)])


def part_ways(x):
    pairs = [(2 * z + c, 2 * ((z + (2, 6)[c]) % 8) + c) for z in range(8) for c in range(2)]
    return lax.ppermute(x, ("z", "core"), pairs)


def gather(x):
    one_above, one_below = shift(x, 7), shift(x, 1)
    two_above, two_below = shift(x, 6), shift(x, 2)
    three_above, three_below = shift(two_above, 7), shift(two_below, 1)
    opposite = shift(two_above, 6)
    return pack(
        [x, one_above, one_below, two_above, two_below, three_above, three_below, opposite]
    )


def body(
    q_latent,
    q_rope,
    latent_cache,
    rope_cache,
    indices,
    w_uv,
    w_out,
    residual,
    norm_gain,
    w_gate,
    w_up,
    w_down,
):
    core = lax.axis_index("core").astype(jnp.int32).reshape(1)
    place = lax.axis_index(HID).astype(jnp.int32).reshape(1)
    height = lax.axis_index("z").astype(jnp.int32).reshape(1)
    gate_other = swap(w_gate)
    up_other = swap(w_up)

    context = attend(indices, q_latent, q_rope, latent_cache, rope_cache)
    moved = exchange(context.reshape(32, 8, LAT), LAYER).reshape(256, LAT)
    flat = gather(heads(core, moved, w_uv))
    other = swap(flat)
    part, mine = project_first(core, height, flat, w_out.T, place, residual.T)
    partial = project(core, height, other, w_out.T, part)
    parts = exchange(partial.reshape(16, 32, -1), HID)
    mid, scaled = middle(parts, mine, norm_gain[None, :])
    scaled = exchange(scaled, HID).reshape(512, 512)
    scaled_other = swap(scaled)
    part = first(core, scaled, w_gate, w_up)
    rest = (core, height, part, scaled, scaled_other, gate_other, up_other)
    opposite, lower, upper = widen((TO_OPPOSITE, TO_LOWER, TO_UPPER), BF16, *rest)
    arrived = (shift(lower, 7), shift(upper, 1), part_ways(opposite))
    (keep,) = widen((TO_KEEP,), F32, *rest)
    stay, lower, upper = merge(core, keep, *arrived)
    hidden = gather(make_hidden(stay, shift(lower, 6), shift(upper, 2)))
    other = swap(hidden).reshape(8, 288, LANES)
    part = down(core, height, hidden.reshape(8, 288, LANES), w_down.T)
    outer = down(core, height, other, w_down.T, part)
    return last(exchange(outer.reshape(16, 32, -1), HID), mid)


def solution(mesh):
    axes = Mesh(mesh.devices.reshape(8, 2, 4, 4), ("z", "core", "y", "x"))
    rows = ("z", "core")
    every = ("z", "core", "y", "x")
    placed = (
        P(every, None, None),
        P(every, None, None),
        P(every, None, None),
        P(every, None, None),
        P(every, None),
        P(HID, None, None),
        P(HID, rows),
        P(None, rows),
        P(rows),
        P(rows, HID),
        P(rows, HID),
        P(HID, rows),
    )
    return jax.shard_map(
        body, mesh=axes, in_specs=placed, out_specs=P(HID, rows), check_vma=False
    )
```

```python
import functools
import math

import jax
import jax.numpy as jnp
from jax import lax
from jax.experimental import pallas as pl
from jax.experimental.pallas import tpu as pltpu
from jax.sharding import Mesh
from jax.sharding import PartitionSpec as P

D = 7168
ROPE = 64
VDIM = 128
LAT = 512
HEADS = 128
CTX = 3072
F32 = jnp.float32
BF16 = jnp.bfloat16
HID = ("y", "x")
LAYER = ("core", "y", "x")
LANES = 128
FAR = (0, 1, 7, 2, 6, 3, 5, 4)
EXP2_SCALE = math.log2(math.e) / math.sqrt(VDIM + ROPE)


def dot(a, b, dims=((1,), (0,))):
    return lax.dot_general(a, b, (dims, ((), ())), preferred_element_type=F32)


def iota(shape, dim):
    return lax.broadcasted_iota(jnp.int32, shape, dim)


def whole(n):
    return [pl.BlockSpec(memory_space=pltpu.VMEM)] * n


def smem():
    return pl.BlockSpec(memory_space=pltpu.SMEM)


def params(mib):
    return pltpu.CompilerParams(vmem_limit_bytes=mib * 2**20)


def cost(flops, nbytes):
    return pl.CostEstimate(flops=flops, bytes_accessed=nbytes, transcendentals=0)


def attend_kernel(idx_ref, ql_ref, qr_ref, lat_ref, rope_ref, out_ref, scores, both):
    seq = pl.program_id(0)
    idx = idx_ref[pl.ds(seq, 1), :]
    high = (iota((32, idx.shape[1]), 0) == lax.shift_right_logical(idx, 7)).astype(F32).astype(BF16)
    low = (iota((LANES, idx.shape[1]), 0) == (idx & 127)).astype(F32).astype(BF16)
    bias = jnp.where(dot(low, high, ((1,), (1,))) > 0.5, 0.0, -1e30)

    q_lat = ql_ref[0]
    q_rope = qr_ref[0]
    step = 1024
    top = jnp.full((8, HEADS), -3e38, F32)
    for at in range(0, CTX, step):
        part = dot(lat_ref[0, at : at + step, :], q_lat, ((1,), (1,)))
        part = part + dot(rope_ref[0, :, at : at + step], q_rope, ((0,), (0,)))
        for j in range(step // LANES):
            g = at // LANES + j
            piece = part[j * LANES : (j + 1) * LANES] + bias[:, g : g + 1]
            scores[g * LANES : (g + 1) * LANES, :] = piece
            top = jnp.maximum(top, jnp.max(piece.reshape(16, 8, HEADS), axis=0))
    peak = jnp.max(top, axis=0, keepdims=True)
    total = jnp.zeros((8, HEADS), F32)
    acc = jnp.zeros((HEADS, LAT), F32)
    for at in range(0, CTX, step):
        e = jnp.exp2((scores[at : at + step, :] - peak) * EXP2_SCALE)
        total = total + jnp.sum(e.reshape(step // 8, 8, HEADS), axis=0)
        acc = acc + dot(e.astype(BF16), lat_ref[0, at : at + step, :], ((0,), (0,)))
    norm = jnp.sum(total, axis=0, keepdims=True)
    same = iota((HEADS, HEADS), 0) == iota((HEADS, HEADS), 1)
    norm = jnp.sum(jnp.where(same, norm, 0.0), axis=1, keepdims=True)
    both[pl.ds(pl.multiple_of(seq * HEADS, HEADS), HEADS), :] = (acc / norm).astype(BF16)

    @pl.when(seq == 1)
    def _():
        row = iota((256, 256), 0)
        col = iota((256, 256), 1)
        i, s, h, c = row & 3, (row >> 2) & 1, (row >> 3) & 15, row >> 7
        pick = (col == s * HEADS + h * 8 + c * 4 + i).astype(F32).astype(BF16)
        out_ref[...] = dot(pick, both[...]).astype(BF16)


def attend(idx, q_lat, q_rope, lat, rope):
    return pl.pallas_call(
        attend_kernel,
        grid=(2,),
        in_specs=[
            pl.BlockSpec(idx.shape, lambda s: (0, 0)),
            pl.BlockSpec((1, HEADS, LAT), lambda s: (s, 0, 0)),
            pl.BlockSpec((1, ROPE, HEADS), lambda s: (s, 0, 0)),
            pl.BlockSpec((1, CTX, LAT), lambda s: (s, 0, 0)),
            pl.BlockSpec((1, ROPE, CTX), lambda s: (s, 0, 0)),
        ],
        out_specs=pl.BlockSpec((256, LAT), lambda s: (0, 0)),
        out_shape=jax.ShapeDtypeStruct((256, LAT), BF16),
        scratch_shapes=[pltpu.VMEM((CTX, HEADS), F32), pltpu.VMEM((256, LAT), BF16)],
        compiler_params=params(58),
        cost_estimate=cost(1_800_000_000, 8_000_000),
        name="attend",
    )(idx, q_lat, q_rope, lat, rope)


def heads_kernel(core_ref, x_ref, w_ref, out_ref):
    core = core_ref[0]
    row = iota((256, 256), 0)
    col = iota((256, 256), 1)
    pick = (col == (row & 63) * 4 + (row >> 6)).astype(F32).astype(BF16)
    sorted_rows = dot(pick, x_ref[...]).astype(BF16)
    for i in range(4):
        part = dot(sorted_rows[i * 64 : (i + 1) * 64], w_ref[core * 4 + i]).astype(BF16)
        out_ref[:, i * VDIM : (i + 1) * VDIM] = part


def heads(core, x, w_uv):
    return pl.pallas_call(
        heads_kernel,
        in_specs=[smem()] + whole(2),
        out_specs=whole(1)[0],
        out_shape=jax.ShapeDtypeStruct((64, 512), BF16),
        compiler_params=params(16),
        cost_estimate=cost(100_000_000, 2_000_000),
        name="heads",
    )(core, x, w_uv)


def pack_kernel(*refs):
    rows = refs[0].shape[0]
    for k, ref in enumerate(refs[:-1]):
        refs[-1][k * rows : (k + 1) * rows] = ref[...]


def pack(blocks):
    rows, columns = blocks[0].shape
    return pl.pallas_call(
        pack_kernel,
        in_specs=whole(8),
        out_specs=whole(1)[0],
        out_shape=jax.ShapeDtypeStruct((8 * rows, columns), BF16),
        compiler_params=params(16),
        cost_estimate=cost(0, 1_000_000),
        name="pack",
    )(*blocks)


def place_chunks(out_ref, z, value):
    for k, far in enumerate(FAR):
        at = pl.multiple_of(lax.rem(z + far, 8) * 64, 64)
        out_ref[pl.ds(at, 64), :] = value[k * 64 : (k + 1) * 64].astype(out_ref.dtype)


def project_kernel(turn, core_ref, z_ref, heads_ref, w_ref, *rest):
    if turn == 0:
        place_ref, res_hbm, out_ref, mine_ref, res_ref, sem = rest
        count = mine_ref.shape[0]
        group = LANES // count
        lanes = pl.multiple_of(place_ref[0] // group * LANES, LANES)
        copy = pltpu.make_async_copy(res_hbm.at[:, pl.ds(lanes, LANES)], res_ref, sem)
        copy.start()
    half = core_ref[0] if turn == 0 else 1 - core_ref[0]
    rows = pl.ds(pl.multiple_of(half * 512, 512), 512)
    total = dot(heads_ref[...], w_ref[:, rows], ((1,), (1,)))
    if turn == 1:
        place_chunks(rest[1], z_ref[0], total + rest[0][...])
    else:
        out_ref[...] = total
        copy.wait()
        begin = lax.rem(place_ref[0], group) * count
        shape = (count, LANES)
        pick = (iota(shape, 1) == iota(shape, 0) + begin).astype(F32).astype(BF16)
        mine_ref[...] = dot(pick, res_ref[...], ((1,), (1,))).astype(BF16)


def project_first(core, z, own, w_out, place, residual):
    cols = w_out.shape[0]
    return pl.pallas_call(
        functools.partial(project_kernel, 0),
        in_specs=[smem(), smem()] + whole(2) + [smem(), pl.BlockSpec(memory_space=pltpu.HBM)],
        out_specs=whole(2),
        out_shape=[
            jax.ShapeDtypeStruct((512, cols), F32),
            jax.ShapeDtypeStruct((32, cols), BF16),
        ],
        scratch_shapes=[pltpu.VMEM((cols, LANES), BF16), pltpu.SemaphoreType.DMA],
        compiler_params=params(16),
        cost_estimate=cost(240_000_000, 2_000_000),
        name="projecta",
    )(core, z, own, w_out, place, residual)


def project(core, z, other, w_out, before):
    return pl.pallas_call(
        functools.partial(project_kernel, 1),
        in_specs=[smem(), smem()] + whole(3),
        out_specs=whole(1)[0],
        out_shape=jax.ShapeDtypeStruct((512, w_out.shape[0]), BF16),
        compiler_params=params(16),
        cost_estimate=cost(240_000_000, 2_000_000),
        name="projectb",
    )(core, z, other, w_out, before)


def middle_kernel(parts_ref, res_ref, gain_ref, mid_ref, out_ref):
    rows, cols = mid_ref.shape
    total = parts_ref[0].astype(F32)
    for k in range(1, parts_ref.shape[0]):
        total = total + parts_ref[k].astype(F32)
    mid = (res_ref[...].astype(F32) + total).astype(BF16)
    mid_ref[...] = mid
    wide = mid.astype(F32)
    squares = jnp.sum(wide * wide, axis=1, keepdims=True)
    upper = squares.astype(BF16).astype(F32)
    lane = iota((rows, 512 - cols), 1)
    extra = jnp.where(lane == 0, upper, jnp.where(lane == 1, squares - upper, 0.0)).astype(BF16)
    scaled = (wide * gain_ref[...].astype(F32)).astype(BF16)
    for k in range(out_ref.shape[0]):
        out_ref[k, :, :cols] = scaled
        out_ref[k, :, cols:] = extra


def middle(parts, residual, gain):
    rows, cols = parts.shape[1:]
    return pl.pallas_call(
        middle_kernel,
        in_specs=whole(3),
        out_specs=whole(2),
        out_shape=[
            jax.ShapeDtypeStruct((rows, cols), BF16),
            jax.ShapeDtypeStruct((16, rows, 512), BF16),
        ],
        compiler_params=params(16),
        cost_estimate=cost(2_500_000_000, 1_500_000),
        name="middle",
    )(parts, residual, gain)


def first_kernel(core_ref, own_ref, g_ref, u_ref, out_ref):
    deep = g_ref.shape[0]
    full = pl.ds(pl.multiple_of(core_ref[0] * 640, LANES), 512)
    own = own_ref[:, :deep]
    out_ref[:, 0:512] = dot(own, g_ref[:, full])
    out_ref[:, 512:1024] = dot(own, u_ref[:, full])
    out_ref[:, 1024:1152] = dot(own, g_ref[:, 512:640])
    out_ref[:, 1152:1280] = dot(own, u_ref[:, 512:640])


def first(core, own, gate, upper):
    return pl.pallas_call(
        first_kernel,
        in_specs=[smem()] + whole(3),
        out_specs=whole(1)[0],
        out_shape=jax.ShapeDtypeStruct((512, 1280), F32),
        compiler_params=params(16),
        cost_estimate=cost(560_000_000, 5_000_000),
        name="first",
    )(core, own, gate, upper)


def widen_kernel(lists, core_ref, z_ref, part_ref, own_ref, other_ref, g_ref, u_ref, *outs):
    deep = g_ref.shape[0]
    low = core_ref[0] == 0
    full = pl.ds(pl.multiple_of(core_ref[0] * 640, LANES), 512)
    wide = outs[0].dtype == F32
    places = []
    source = 0
    for out_ref, takes in zip(outs, lists):
        at = 0
        for far, begin, rows in takes:
            places.append((out_ref, at, source, far, begin, rows))
            at += 9 * rows + 16
            source += rows

    def rows_of(ref, columns):
        pieces = []
        for _, _, _, far, begin, rows in places:
            at = lax.rem(z_ref[0] + far, 8) * 64 + begin
            pieces.append(ref[pl.ds(pl.multiple_of(at, 32), rows), columns])
        return jnp.concatenate(pieces, axis=0)

    other = rows_of(other_ref, slice(0, deep))

    def put(block, value):
        value = value.astype(outs[0].dtype)
        for out_ref, at, source, _, _, rows in places:
            for j in range(value.shape[1] // LANES):
                begin = at + (block + j) * rows
                out_ref[begin : begin + rows] = value[
                    source : source + rows, j * LANES : (j + 1) * LANES
                ]

    put(0, rows_of(part_ref, slice(0, 512)) + dot(other, g_ref[:, full]))
    put(4, rows_of(part_ref, slice(512, 1024)) + dot(other, u_ref[:, full]))
    gate = rows_of(part_ref, slice(1024, 1152)) + dot(other, g_ref[:, 512:640])
    upper = rows_of(part_ref, slice(1152, 1280)) + dot(other, u_ref[:, 512:640])
    straight = jnp.where(low, gate, upper)
    turned = pltpu.roll(jnp.where(low, upper, gate), 64, 1)
    lane = iota(gate.shape, 1)
    begin = jnp.where(low, 0, 64)
    put(8, jnp.where((lane >= begin) & (lane < begin + 64), straight, turned))
    extra = slice(deep, 512)
    squares = jnp.sum(rows_of(own_ref, extra).astype(F32), axis=1, keepdims=True)
    squares = squares + jnp.sum(rows_of(other_ref, extra).astype(F32), axis=1, keepdims=True)
    for out_ref, at, source, _, first_row, rows in places:
        same = iota((rows, LANES), 0) + first_row == iota((rows, LANES), 1)
        line = jnp.where(same, squares[source : source + rows], 0.0)
        line = jnp.sum(line, axis=0, keepdims=True)
        out_ref[at + 9 * rows : at + 9 * rows + 16] = tile_of(line, wide).astype(out_ref.dtype)


def tile_of(line, wide):
    row = iota((16, LANES), 0)
    high = line if wide else line.astype(BF16).astype(F32)
    return jnp.where(row == 0, high, jnp.where(row == 1, line - high, 0.0))


def widen(lists, kind, core, z, part, own, other, gate, upper):
    shapes = [
        jax.ShapeDtypeStruct((sum(9 * n + 16 for _, _, n in takes), LANES), kind) for takes in lists
    ]
    return pl.pallas_call(
        functools.partial(widen_kernel, lists),
        in_specs=[smem(), smem()] + whole(5),
        out_specs=whole(len(lists)),
        out_shape=shapes,
        compiler_params=params(16),
        cost_estimate=cost(200_000_000, 6_000_000),
        name="widen",
    )(core, z, part, own, other, gate, upper)


BLOCK = 592
TO_LOWER = ((7, 0, 64), (5, 0, 64))
TO_UPPER = ((1, 0, 64), (3, 0, 64))
TO_OPPOSITE = ((4, 0, 64),)
TO_KEEP = ((0, 0, 64), (6, 0, 64), (2, 0, 64))


def merge_kernel(core_ref, keep_ref, above_ref, below_ref, far_ref, stay_ref, down_ref, up_ref):
    def block(ref, k):
        return ref[k * BLOCK : (k + 1) * BLOCK].astype(F32)

    stay_ref[...] = block(keep_ref, 0) + block(above_ref, 0) + block(below_ref, 0)
    far = far_ref[...].astype(F32)
    for out_ref, k, near_ref, goes in (
        (down_ref, 1, above_ref, core_ref[0] == 1),
        (up_ref, 2, below_ref, core_ref[0] == 0),
    ):
        total = block(keep_ref, k) + block(near_ref, 1) + jnp.where(goes, far, 0.0)
        out_ref[:576] = total[:576].astype(BF16)
        line = jnp.sum(total[576:], axis=0, keepdims=True)
        out_ref[576:] = tile_of(line, False).astype(BF16)


def merge(core, *parts):
    shapes = [jax.ShapeDtypeStruct((BLOCK, LANES), kind) for kind in (F32, BF16, BF16)]
    return pl.pallas_call(
        merge_kernel,
        in_specs=[smem()] + whole(4),
        out_specs=whole(3),
        out_shape=shapes,
        compiler_params=params(16),
        cost_estimate=cost(5_000_000, 3_000_000),
        name="merge",
    )(core, *parts)


def gated(gate, upper):
    return gate / (1.0 + jnp.exp(-gate)) * upper


def hidden_kernel(stay_ref, above_ref, below_ref, out_ref):
    chunk = 64

    def total(at, rows):
        value = above_ref[at : at + rows].astype(F32) + below_ref[at : at + rows].astype(F32)
        return stay_ref[at : at + rows] + value

    line = jnp.sum(total(576, 16), axis=0, keepdims=True)
    same = iota((chunk, LANES), 0) == iota((chunk, LANES), 1)
    squares = jnp.sum(jnp.where(same, line, 0.0), axis=1, keepdims=True)
    rstd = lax.rsqrt(squares / D + 1e-06)

    def put(at, value):
        out_ref[at : at + value.shape[0]] = value.astype(BF16)

    for j in range(4):
        gate = total(j * chunk, chunk) * rstd
        put(j * chunk, gated(gate, total((4 + j) * chunk, chunk) * rstd))
    mixed = total(8 * chunk, chunk) * rstd
    value = gated(mixed, pltpu.roll(mixed, 64, 1))
    lane = iota((32, LANES), 1)
    put(256, jnp.where(lane < 64, value[:32], pltpu.roll(value[32:], 64, 1)))


def make_hidden(stay, above, below):
    return pl.pallas_call(
        hidden_kernel,
        in_specs=whole(3),
        out_specs=whole(1)[0],
        out_shape=jax.ShapeDtypeStruct((288, LANES), BF16),
        compiler_params=params(16),
        cost_estimate=cost(5_000_000, 2_000_000),
        name="hidden",
    )(stay, above, below)


def down_kernel(turn, core_ref, z_ref, units_ref, w_ref, *rest):
    core = core_ref[0] if turn == 0 else 1 - core_ref[0]
    low = core == 0
    rows = pl.ds(pl.multiple_of(core * 640, LANES), 512)
    blocks = [units_ref[:, j * 64 : (j + 1) * 64].reshape(512, LANES) for j in range(4)]
    total = dot(jnp.concatenate(blocks, axis=1), w_ref[:, rows], ((1,), (1,)))
    packed = units_ref[:, 256:288].astype(F32).reshape(256, LANES)
    turned = pltpu.roll(packed, 64, 1)
    lane = iota(packed.shape, 1)
    begin = jnp.where(low, 0, 64)
    here = (lane >= begin) & (lane < begin + 64)
    top = jnp.where(here, jnp.where(low, packed, turned), 0.0).reshape(8, 32, LANES)
    bottom = jnp.where(here, jnp.where(low, turned, packed), 0.0).reshape(8, 32, LANES)
    mixed = jnp.concatenate([top, bottom], axis=1).reshape(512, LANES).astype(BF16)
    total = total + dot(mixed, w_ref[:, 512:640], ((1,), (1,)))
    if turn == 1:
        place_chunks(rest[1], z_ref[0], total + rest[0][...])
    else:
        rest[0][...] = total


def down(core, z, units, w_down, before=None):
    turn = 0 if before is None else 1
    return pl.pallas_call(
        functools.partial(down_kernel, turn),
        in_specs=[smem(), smem()] + whole(2 + turn),
        out_specs=whole(1)[0],
        out_shape=jax.ShapeDtypeStruct((512, w_down.shape[0]), BF16 if turn else F32),
        compiler_params=params(16),
        cost_estimate=cost(280_000_000, 2_000_000),
        name="down" + "ab"[turn],
    )(core, z, units, w_down, *([before] if turn else []))


def last_kernel(parts_ref, mid_ref, out_ref):
    total = parts_ref[0].astype(F32)
    for k in range(1, parts_ref.shape[0]):
        total = total + parts_ref[k].astype(F32)
    out_ref[...] = (mid_ref[...].astype(F32) + total).astype(BF16)


def last(parts, mid):
    return pl.pallas_call(
        last_kernel,
        in_specs=whole(2),
        out_specs=whole(1)[0],
        out_shape=jax.ShapeDtypeStruct(mid.shape, BF16),
        compiler_params=params(16),
        cost_estimate=cost(1_000_000, 1_000_000),
        name="last",
    )(parts, mid)


def exchange(x, axes):
    return lax.all_to_all(x, axes, split_axis=0, concat_axis=0, tiled=True)


def swap(x):
    return lax.ppermute(x, "core", [(0, 1), (1, 0)])


def shift(x, far):
    return lax.ppermute(x, "z", [(i, (i + far) % 8) for i in range(8)])


def part_ways(x):
    pairs = [(2 * z + c, 2 * ((z + (2, 6)[c]) % 8) + c) for z in range(8) for c in range(2)]
    return lax.ppermute(x, ("z", "core"), pairs)


def gather(x):
    one_above, one_below = shift(x, 7), shift(x, 1)
    two_above, two_below = shift(x, 6), shift(x, 2)
    three_above, three_below = shift(two_above, 7), shift(two_below, 1)
    opposite = part_ways(jnp.where(lax.axis_index("core") == 0, two_below, two_above))
    return pack(
        [x, one_above, one_below, two_above, two_below, three_above, three_below, opposite]
    )


def body(
    q_latent,
    q_rope,
    latent_cache,
    rope_cache,
    indices,
    w_uv,
    w_out,
    residual,
    norm_gain,
    w_gate,
    w_up,
    w_down,
):
    core = lax.axis_index("core").astype(jnp.int32).reshape(1)
    place = lax.axis_index(HID).astype(jnp.int32).reshape(1)
    height = lax.axis_index("z").astype(jnp.int32).reshape(1)
    gate_other = swap(w_gate)
    up_other = swap(w_up)

    context = attend(indices, q_latent, q_rope, latent_cache, rope_cache)
    moved = exchange(context.reshape(32, 8, LAT), LAYER).reshape(256, LAT)
    flat = gather(heads(core, moved, w_uv))
    other = swap(flat)
    part, mine = project_first(core, height, flat, w_out.T, place, residual.T)
    partial = project(core, height, other, w_out.T, part)
    parts = exchange(partial.reshape(16, 32, -1), HID)
    mid, scaled = middle(parts, mine, norm_gain[None, :])
    scaled = exchange(scaled, HID).reshape(512, 512)
    scaled_other = swap(scaled)
    part = first(core, scaled, w_gate, w_up)
    rest = (core, height, part, scaled, scaled_other, gate_other, up_other)
    opposite, lower, upper = widen((TO_OPPOSITE, TO_LOWER, TO_UPPER), BF16, *rest)
    arrived = (shift(lower, 7), shift(upper, 1), part_ways(opposite))
    (keep,) = widen((TO_KEEP,), F32, *rest)
    stay, lower, upper = merge(core, keep, *arrived)
    hidden = gather(make_hidden(stay, shift(lower, 6), shift(upper, 2)))
    other = swap(hidden).reshape(8, 288, LANES)
    part = down(core, height, hidden.reshape(8, 288, LANES), w_down.T)
    outer = down(core, height, other, w_down.T, part)
    return last(exchange(outer.reshape(16, 32, -1), HID), mid)


def solution(mesh):
    axes = Mesh(mesh.devices.reshape(8, 2, 4, 4), ("z", "core", "y", "x"))
    rows = ("z", "core")
    every = ("z", "core", "y", "x")
    placed = (
        P(every, None, None),
        P(every, None, None),
        P(every, None, None),
        P(every, None, None),
        P(every, None),
        P(HID, None, None),
        P(HID, rows),
        P(None, rows),
        P(rows),
        P(rows, HID),
        P(rows, HID),
        P(HID, rows),
    )
    return jax.shard_map(
        body, mesh=axes, in_specs=placed, out_specs=P(HID, rows), check_vma=False
    )
```
